128 devices in a mesh: dp: 4 (over x), vocab: 32 (over z, y, core).
Axes of the slice: x: 4, y: 4, z: 4, core: 2. Of those that a mesh axis runs over, the one named last changes fastest.
Arguments:
- hidden: bfloat16 [2048, 3584], P('dp'), may hold values from -120 to 120
- head_weight: bfloat16 [3584, 76032], P(None, 'vocab'), may hold values from -0.09375 to 0.09375
- teacher_ids: int32 [2048, 64], P(('dp', 'vocab')), may hold values from 0 to 76031, as said below
- teacher_logits: float32 [2048, 64], P(('dp', 'vocab')), may hold values from -400 to 400
Outputs:
- token_loss: float32 [2048], P('dp')
- grad_hidden: float32 [2048, 3584], P(('dp', 'vocab'))
The draws below stay inside these ranges and needn't reach their ends.
Inputs may be any that keep to these rules, and one draw needn't show every extreme that they name: `teacher_ids`: each row holds 64 distinct ids in ascending order.
All inputs are finite; a program needn't handle non-finite values.
Results may differ from the reference program's by a relative error of at most 0.0029.
Values sent between devices are 32-bit elements; how exact they have to be, the bound alone decides.
A program may use at most 128 MiB of HBM per device.

```python
import jax
import jax.numpy as jnp
from jax import lax

D = 3584
V = 76032
K = 64
TOKENS = 2048
N_VOCAB = 32


def draw_hidden(key, part):
    key = jax.random.fold_in(key, 11)
    first_key = jax.random.fold_in(key, 0)
    return jnp.clip(jax.random.normal(first_key, (TOKENS, D), jnp.float32), -6.0, 6.0).astype(jnp.bfloat16)


def draw_teacher_logits(key, part):
    key = jax.random.fold_in(key, 23)
    first_key = jax.random.fold_in(key, 0)
    return 0.5 * jnp.clip(jax.random.normal(first_key, (TOKENS, K), jnp.float32), -6.0, 6.0)


def draw_teacher_ids(key, part):
    key = jax.random.fold_in(key, 37)
    first_key, second_key, third_key, fourth_key = jax.random.split(key, 4)
    strata = 2 * K
    stride = V // strata
    scores = jax.random.randint(first_key, (TOKENS, strata), 0, 65536) * strata + jnp.arange(strata, dtype=jnp.int32)[None, :]
    order = jnp.argsort(scores, axis=1, stable=True)
    chosen = jnp.sort(order[:, :K], axis=1).astype(jnp.int32)
    inner = jax.random.randint(second_key, (TOKENS, K), 0, stride)
    spread_ids = chosen * stride + inner
    window_start = jax.random.randint(third_key, (TOKENS, 1), 0, V - strata + 1)
    packed_ids = window_start + chosen
    clustered = jax.random.randint(fourth_key, (TOKENS, 1), 0, 4) == 0
    return jnp.where(clustered, packed_ids, spread_ids).astype(jnp.int32)


def block_levels(own_key, extent, cuts, least, largest):
    def one(position, blocks):
        steps = jax.random.uniform(jax.random.fold_in(jax.random.fold_in(own_key, 6), position), (blocks,), jnp.float32, least / len(cuts), largest / len(cuts))
        return jnp.repeat(jnp.exp(steps), extent[position] // blocks).reshape((-1,) + (1,) * (len(extent) - position - 1))

    level = one(*cuts[0])
    for cut in cuts[1:]:
        level = level * one(*cut)
    return level


def bell_draw(stream_key, dims, width, limit, shards=(), kind=jnp.bfloat16):
    factor_of = block_levels(stream_key, dims, shards, -0.22, 0.18) if shards else 1.0
    drawn = jax.random.normal(stream_key, dims, jnp.float32) * width * factor_of
    return jnp.minimum(jnp.maximum(drawn, -limit), limit).astype(kind)


def setup_inputs(seed: int = 0) -> dict:
    keys = jax.random.split(jax.random.key(seed), 5)
    hidden = draw_hidden(jax.random.fold_in(keys[4], 71), 0)
    head_weight = bell_draw(keys[1], (D, V), D ** -0.5, 0.09375, ((1, 32),))
    teacher_ids = draw_teacher_ids(jax.random.fold_in(keys[4], 71), 0)
    teacher_logits = draw_teacher_logits(jax.random.fold_in(keys[4], 71), 0)
    return {"hidden": hidden, "head_weight": head_weight, "teacher_ids": teacher_ids, "teacher_logits": teacher_logits}


def teacher_side(teacher_logits):
    shifted = teacher_logits - jnp.max(teacher_logits, axis=1, keepdims=True)
    log_probs = shifted - jnp.log(jnp.sum(jnp.exp(shifted), axis=1, keepdims=True))
    probs = jnp.exp(log_probs)
    return probs, jnp.sum(probs * log_probs, axis=1)


def local_index(teacher_ids, probs, offset, columns):
    local_ids = teacher_ids - offset
    inside = (local_ids >= 0) & (local_ids < columns)
    safe_index = jnp.where(inside, local_ids, 0).astype(jnp.int32)
    weights = jnp.where(inside, probs, jnp.zeros_like(probs))
    return safe_index, weights


def cross_terms(logits, safe_index, weights):
    picked = jnp.take_along_axis(logits, safe_index, axis=1)
    return jnp.sum(weights * picked, axis=1)


def make_target(logits, safe_index, weights):
    row_index = jnp.arange(logits.shape[0], dtype=jnp.int32)[:, None]
    return jnp.zeros_like(logits).at[row_index, safe_index].add(weights)


def reference(hidden, head_weight, teacher_ids, teacher_logits):
    probs, negent = teacher_side(teacher_logits)
    columns = V // N_VOCAB
    rows_all = hidden.shape[0]

    def block_logits(block_index):
        offset = (block_index * columns).astype(jnp.int32)
        weight_block = lax.dynamic_slice_in_dim(head_weight, offset, columns, 1)
        logits = jnp.dot(hidden, weight_block, preferred_element_type=jnp.float32)
        return offset, weight_block, logits

    def first_pass(block_index, carry):
        running_max, running_sum, cross = carry
        offset, weight_block, logits = block_logits(block_index)
        safe_index, weights = local_index(teacher_ids, probs, offset, columns)
        new_max = jnp.maximum(running_max, jnp.max(logits, axis=1))
        running_sum = running_sum * jnp.exp(running_max - new_max) + jnp.sum(jnp.exp(logits - new_max[:, None]), axis=1)
        return new_max, running_sum, cross + cross_terms(logits, safe_index, weights)

    start = (jnp.full((rows_all,), -jnp.inf, jnp.float32), jnp.zeros((rows_all,), jnp.float32), jnp.zeros((rows_all,), jnp.float32))
    running_max, running_sum, cross = lax.fori_loop(0, N_VOCAB, first_pass, start)
    log_total = running_max + jnp.log(running_sum)
    token_loss = negent - cross + log_total

    def second_pass(block_index, total):
        offset, weight_block, logits = block_logits(block_index)
        safe_index, weights = local_index(teacher_ids, probs, offset, columns)
        target = make_target(logits, safe_index, weights)
        grad_logits = (jnp.exp(logits - log_total[:, None]) - target).astype(jnp.bfloat16)
        return total + lax.dot_general(grad_logits, weight_block, (((1,), (1,)), ((), ())), preferred_element_type=jnp.float32)

    grad_hidden = lax.fori_loop(0, N_VOCAB, second_pass, jnp.zeros((rows_all, D), jnp.float32))
    return token_loss, grad_hidden
```

```python
import functools

import jax
import jax.numpy as jnp
from jax import lax
from jax.experimental import pallas as pl
from jax.experimental.pallas import tpu as pltpu
from jax.sharding import PartitionSpec as P

MESH = pl.DeviceIdType.MESH
NV = 32
TOK = 512
HALF = 256
OWN = 16
D = 3584
COLS = 2376
MAIN = 2304
TAIL = COLS - MAIN
PADDED = MAIN + 128
TILES = PADDED // 128
DEPTH = 512
NB = D // DEPTH
CW = 512
NC = D // CW
K = 64
NT = (((1,), (1,)), ((), ()))


def slot_of(index):
    core, y, z = index % 2, (index // 2) % 4, index // 8
    return core * 16 + (y * 4 + z) * (1 - core) + (z * 4 + y) * core


def kernel(
    hidden, weight, ids_ref, tlog_ref,
    grad_out, loss_out,
    w, h, logits, target, gm, gt, g, cr, r11, r12, r21, r22,
    comb, stats, ltcol, lsecol, crosscol,
    h_sem, w_sem, comb_send, comb_recv, st_send, st_recv,
    c_send, c_recv, p_send, p_recv,
):
    me = lax.axis_index("vocab")
    core = me % 2
    y = (me // 2) % 4
    z = me // 8
    a = y * (1 - core) + z * core
    b = z * (1 - core) + y * core
    stride_a = 1 + 3 * core
    stride_b = 4 - 3 * core

    def device(a_pos, b_pos):
        return {"vocab": (a_pos * stride_a + b_pos * stride_b) * 2 + core}

    mate = {"vocab": me + 1 - 2 * core}
    a_right, a_left = (a + 1) % 4, (a + 3) % 4
    b_right, b_left = (b + 1) % 4, (b + 3) % 4
    my_slot = core * 16 + a * 4 + b

    for v in range(NV):
        s = slot_of(v)
        pltpu.make_async_copy(hidden.at[pl.ds(v * OWN, OWN)], h.at[pl.ds(s * OWN, OWN)], h_sem).start()

    def w_copy(n):
        rows = pl.ds(n * DEPTH, DEPTH)
        return pltpu.make_async_copy(weight.at[rows], w.at[rows], w_sem.at[n])

    for n in range(NB):
        w_copy(n).start()

    barrier = pltpu.get_barrier_semaphore()
    for d in range(1, NV):
        pl.semaphore_signal(barrier, inc=1, device_id={"vocab": (me + d) % NV}, device_id_type=MESH)
    tl = tlog_ref[...]
    shifted = tl - jnp.max(tl, axis=1, keepdims=True)
    log_probs = shifted - jnp.log(jnp.sum(jnp.exp(shifted), axis=1, keepdims=True))
    probs = jnp.exp(log_probs)
    negent = jnp.sum(probs * log_probs, axis=1, keepdims=True)
    comb[my_slot] = jnp.concatenate([ids_ref[...].astype(jnp.float32), probs], axis=1)
    pl.semaphore_wait(barrier, NV - 1)

    def comb_copy(d):
        return pltpu.make_async_remote_copy(
            comb.at[my_slot], comb.at[my_slot], comb_send, comb_recv,
            device_id={"vocab": (me + d) % NV}, device_id_type=MESH)

    for d in range(1, NV):
        comb_copy(d).start()

    pltpu.make_async_copy(h, h, h_sem).wait()

    for n in range(NB):
        w_copy(n).wait()
        deep = slice(n * DEPTH, (n + 1) * DEPTH)

        @pl.loop(0, MAIN // 256)
        def _(k):
            cols = pl.ds(pl.multiple_of(k * 256, 256), 256)
            part = jnp.dot(h[:, deep], w[deep, cols], preferred_element_type=jnp.float32)
            logits[:, cols] = part if n == 0 else logits[:, cols] + part

        part = jnp.dot(h[:, deep], w[deep, MAIN:], preferred_element_type=jnp.float32)
        logits[:, MAIN:COLS] = part if n == 0 else logits[:, MAIN:COLS] + part

    lane = lax.broadcasted_iota(jnp.int32, (8, 128), 1)

    @pl.loop(0, TOK // 8, unroll=4)
    def _(i):
        rows = pl.ds(pl.multiple_of(i * 8, 8), 8)
        tiles = [logits[rows, t * 128:(t + 1) * 128] for t in range(TILES)]
        tiles[-1] = jnp.where(lane < TAIL, tiles[-1], jnp.float32(-1e30))
        top = functools.reduce(jnp.maximum, tiles)
        m = jnp.max(top, axis=1, keepdims=True)
        acc = functools.reduce(jnp.add, [jnp.exp(t - m) for t in tiles])
        s = jnp.sum(acc, axis=1, keepdims=True)
        lsecol[rows, :] = jnp.broadcast_to(m + jnp.log(s), (8, 128))

    def original_rows(col, i):
        return jnp.concatenate([col[pl.ds(slot_of(8 * i + j) * OWN, OWN), :] for j in range(8)], axis=0)

    for i in range(4):
        stats[0, my_slot, pl.ds(i, 1), :] = jnp.transpose(original_rows(lsecol, i))[0:1, :]

    def stat_copy(k, d):
        return pltpu.make_async_remote_copy(
            stats.at[k, my_slot], stats.at[k, my_slot], st_send.at[k], st_recv.at[k],
            device_id={"vocab": (me + d) % NV}, device_id_type=MESH)

    for d in range(1, NV):
        stat_copy(0, d).start()

    pltpu.make_async_copy(comb.at[0:NV - 1], comb.at[0:NV - 1], comb_recv).wait()
    first = (me * COLS).astype(jnp.float32)
    lane_f = lane.astype(jnp.float32)

    def pick(table, pos):
        return jnp.take_along_axis(table, pos, axis=1)

    @pl.loop(0, TOK // 8)
    def _(i):
        rows = pl.ds(pl.multiple_of(i * 8, 8), 8)
        table = comb[i // 2, pl.ds(pl.multiple_of((i % 2) * 8, 8), 8), :]
        shape = (8, 128)
        mid = jnp.broadcast_to(table[:, 31:32], shape)
        low = jnp.broadcast_to(table[:, 15:16], shape)
        high = jnp.broadcast_to(table[:, 47:48], shape)
        cross = jnp.zeros(shape, jnp.float32)
        for t in range(TILES):
            col = lane_f + (first + jnp.float32(t * 128))
            c = mid < col
            pos = jnp.where(c, 32, 0)
            probe = jnp.where(c, high, low)
            pos = pos + jnp.where(probe < col, 16, 0)
            for s in (8, 4, 2, 1):
                probe = pick(table, pos + (s - 1))
                pos = pos + jnp.where(probe < col, s, 0)
            hit = pick(table, pos) == col
            if t == TILES - 1:
                hit = hit & (lane < TAIL)
            value = jnp.where(hit, pick(table, pos + K), jnp.float32(0.0))
            target[rows, t * 128:(t + 1) * 128] = value
            cross = cross + value * logits[rows, t * 128:(t + 1) * 128]
        crosscol[rows, :] = jnp.broadcast_to(jnp.sum(cross, axis=1, keepdims=True), shape)

    own_rows = pl.ds(pl.multiple_of(my_slot * OWN, OWN), OWN)
    crosscol[own_rows, :] = crosscol[own_rows, :] - negent
    for i in range(4):
        stats[1, my_slot, pl.ds(i, 1), :] = jnp.transpose(original_rows(crosscol, i))[0:1, :]
    for d in range(1, NV):
        stat_copy(1, d).start()

    pltpu.make_async_copy(stats.at[0, 0:NV - 1], stats.at[0, 0:NV - 1], st_recv.at[0]).wait()
    lse = stats[0]
    top = jnp.max(lse, axis=0)
    log_total = top + jnp.log(jnp.sum(jnp.exp(lse - top[None]), axis=0))
    for i in range(4):
        col = jnp.transpose(jnp.broadcast_to(log_total[i:i + 1, :], (128, 128)))
        for j in range(8):
            ltcol[pl.ds(slot_of(8 * i + j) * OWN, OWN), :] = col[j * OWN:(j + 1) * OWN, :]

    lane16 = lax.broadcasted_iota(jnp.int32, (16, 128), 1)

    def make_grad(which):
        @pl.loop(0, HALF // 16)
        def _(i):
            rows = pl.ds(pl.multiple_of(which * HALF + i * 16, 16), 16)
            here = pl.ds(pl.multiple_of(i * 16, 16), 16)
            lt = ltcol[rows, :]
            for t in range(TILES):
                at = slice(t * 128, (t + 1) * 128)
                value = jnp.exp(logits[rows, at] - lt) - target[rows, at]
                if t == TILES - 1:
                    gt[which, here, :] = jnp.where(lane16 < TAIL, value, jnp.float32(0.0)).astype(jnp.bfloat16)
                else:
                    gm[which, here, at] = value.astype(jnp.bfloat16)

    def multiply(c, which):
        @pl.loop(0, CW // 256)
        def _(k):
            rows = pl.ds(pl.multiple_of(c * CW + k * 256, 256), 256)
            part = lax.dot_general(gm[which], w[rows, 0:MAIN], NT, preferred_element_type=jnp.float32)
            part = part + lax.dot_general(gt[which, :, 0:TAIL], w[rows, MAIN:COLS], NT, preferred_element_type=jnp.float32)
            g[c, which, :, :, :, pl.ds(pl.multiple_of(k * 256, 256), 256)] = part.reshape(4, 4, OWN, 256)

    make_grad(1 - core)
    make_grad(core)

    def remote(src, dst, send, recv, where):
        return pltpu.make_async_remote_copy(src, dst, send, recv, device_id=where, device_id_type=MESH)

    def core_copy(c):
        return remote(g.at[c, 1 - core], cr.at[c], c_send.at[c], c_recv.at[c], mate)

    def step11(c):
        far = (a + 2) % 4
        return (
            remote(g.at[c, core, far, 0:2], r11.at[c, 0], p_send.at[c, 0], p_recv.at[c, 0], device(a_right, b)),
            remote(g.at[c, core, far, 2:4], r11.at[c, 1], p_send.at[c, 1], p_recv.at[c, 1], device(a_left, b)),
        )

    def step12(c):
        return (
            remote(g.at[c, core, a_right], r12.at[c, 0], p_send.at[c, 2], p_recv.at[c, 2], device(a_right, b)),
            remote(g.at[c, core, a_left], r12.at[c, 1], p_send.at[c, 3], p_recv.at[c, 3], device(a_left, b)),
        )

    def step21(c):
        far = (b + 2) % 4
        return (
            remote(g.at[c, core, a, far, 0:8], r21.at[c, 0], p_send.at[c, 4], p_recv.at[c, 4], device(a, b_right)),
            remote(g.at[c, core, a, far, 8:16], r21.at[c, 1], p_send.at[c, 5], p_recv.at[c, 5], device(a, b_left)),
        )

    def step22(c):
        return (
            remote(g.at[c, core, a, b_right], r22.at[c, 0], p_send.at[c, 6], p_recv.at[c, 6], device(a, b_right)),
            remote(g.at[c, core, a, b_left], r22.at[c, 1], p_send.at[c, 7], p_recv.at[c, 7], device(a, b_left)),
        )

    def start(copies):
        for copy in copies:
            copy.start()

    def arrived(copies):
        for copy in copies:
            copy.wait_recv()

    def when(i, lag):
        return pl.when((i >= lag) & (i < NC + lag))

    @pl.loop(0, NC + 5)
    def _(i):
        @when(i, 0)
        def _():
            multiply(i, 1 - core)
            core_copy(i).start()
            multiply(i, core)

        @when(i, 1)
        def _():
            c = i - 1
            core_copy(c).wait_recv()
            for k in range(4):
                g[c, core, k] = g[c, core, k] + cr[c, k]
            start(step11(c))

        @when(i, 2)
        def _():
            c = i - 2
            arrived(step11(c))
            g[c, core, a_right, 0:2] = g[c, core, a_right, 0:2] + r11[c, 0]
            g[c, core, a_left, 2:4] = g[c, core, a_left, 2:4] + r11[c, 1]
            start(step12(c))

        @when(i, 3)
        def _():
            c = i - 3
            arrived(step12(c))
            g[c, core, a] = g[c, core, a] + (r12[c, 0] + r12[c, 1])
            start(step21(c))

        @when(i, 4)
        def _():
            c = i - 4
            arrived(step21(c))
            g[c, core, a, b_right, 0:8] = g[c, core, a, b_right, 0:8] + r21[c, 0]
            g[c, core, a, b_left, 8:16] = g[c, core, a, b_left, 8:16] + r21[c, 1]
            start(step22(c))

        @when(i, 5)
        def _():
            c = i - 5
            arrived(step22(c))
            grad_out[:, pl.ds(pl.multiple_of(c * CW, CW), CW)] = g[c, core, a, b] + (r22[c, 0] + r22[c, 1])

    pltpu.make_async_copy(stats.at[1, 0:NV - 1], stats.at[1, 0:NV - 1], st_recv.at[1]).wait()
    loss_out[...] = log_total - jnp.sum(stats[1], axis=0)

    pltpu.make_async_copy(comb.at[0:NV - 1], comb.at[0:NV - 1], comb_send).wait()
    for k in range(2):
        pltpu.make_async_copy(stats.at[k, 0:NV - 1], stats.at[k, 0:NV - 1], st_send.at[k]).wait()

    @pl.loop(0, NC)
    def _(c):
        core_copy(c).wait_send()
        for copy in step11(c) + step12(c) + step21(c) + step22(c):
            copy.wait_send()


def local(hidden, head_weight, teacher_ids, teacher_logits):
    any_space = pl.BlockSpec(memory_space=pl.ANY)
    vmem = pl.BlockSpec(memory_space=pltpu.VMEM)
    f32, bf16 = jnp.float32, jnp.bfloat16
    dma = pltpu.SemaphoreType.DMA
    grad, loss = pl.pallas_call(
        kernel,
        out_shape=(jax.ShapeDtypeStruct((OWN, D), f32), jax.ShapeDtypeStruct((4, 128), f32)),
        in_specs=[any_space, any_space, vmem, vmem],
        out_specs=(vmem, vmem),
        scratch_shapes=[
            pltpu.VMEM((D, COLS), bf16),
            pltpu.VMEM((TOK, D), bf16),
            pltpu.VMEM((TOK, PADDED), f32),
            pltpu.VMEM((TOK, PADDED), f32),
            pltpu.VMEM((2, HALF, MAIN), bf16),
            pltpu.VMEM((2, HALF, 128), bf16),
            pltpu.VMEM((NC, 2, 4, 4, OWN, CW), f32),
            pltpu.VMEM((NC, 4, 4, OWN, CW), f32),
            pltpu.VMEM((NC, 2, 2, OWN, CW), f32),
            pltpu.VMEM((NC, 2, 4, OWN, CW), f32),
            pltpu.VMEM((NC, 2, 8, CW), f32),
            pltpu.VMEM((NC, 2, OWN, CW), f32),
            pltpu.VMEM((NV, OWN, 128), f32),
            pltpu.VMEM((2, NV, 4, 128), f32),
            pltpu.VMEM((TOK, 128), f32),
            pltpu.VMEM((TOK, 128), f32),
            pltpu.VMEM((TOK, 128), f32),
            dma, dma((NB,)), dma, dma, dma((2,)), dma((2,)),
            dma((NC,)), dma((NC,)), dma((NC, 8)), dma((NC, 8)),
        ],
        compiler_params=pltpu.CompilerParams(
            collective_id=0, has_side_effects=True, vmem_limit_bytes=60 * 1024 * 1024),
    )(hidden, head_weight, teacher_ids, teacher_logits)
    return loss.reshape(TOK), grad


def solution(mesh):
    placed = (P("dp", None), P(None, "vocab"), P(("dp", "vocab"), None), P(("dp", "vocab"), None))
    return jax.shard_map(
        local,
        mesh=mesh,
        in_specs=placed,
        out_specs=(P("dp"), P(("dp", "vocab"), None)),
        check_vma=False,
    )
```

```python
import functools

import jax
import jax.numpy as jnp
from jax import lax
from jax.experimental import pallas as pl
from jax.experimental.pallas import tpu as pltpu
from jax.sharding import PartitionSpec as P

MESH = pl.DeviceIdType.MESH
NV = 32
TOK = 512
OWN = 16
D = 3584
COLS = 2376
MAIN = 2304
TAIL = COLS - MAIN
PADDED = MAIN + 128
TILES = PADDED // 128
NB = MAIN // 256
UNIT = 256
CHUNKS = (1, 2, 3, 3, 3, 2)
NC = len(CHUNKS)
K = 64
ORDER = (
    "m", "C0", "m", "m", "C1", "X0", "m", "m", "X1", "m", "C2", "m", "Y0", "m", "X2", "m", "C3",
    "Y1", "m", "m", "X3", "Y2", "m", "C4", "Z0", "m", "X4", "Y3", "Z1", "m", "C5", "K1", "Z2", "X5",
    "K2", "Y4", "F0", "K3", "F1", "Z3", "Y5", "K4", "F2", "Z4", "F3", "Z5", "F4", "F5",
)
NT = (((1,), (1,)), ((), ()))


def slot_of(index):
    core, y, z = index % 2, (index // 2) % 4, index // 8
    return core * 16 + (y * 4 + z) * (1 - core) + (z * 4 + y) * core


def kernel(
    hidden, weight, ids_ref, tlog_ref,
    grad_out, loss_out,
    w, h, logits, target, gm, g, cr, r11, r12, r2,
    comb, stat_core, stat_y, stat_z, ltcol, lsecol, crosscol,
    h_sem, w_sem, comb_send, comb_recv, st_send, st_recv, g_send, g_recv,
):
    me = lax.axis_index("vocab")
    core = me % 2
    y = (me // 2) % 4
    z = me // 8
    a = y * (1 - core) + z * core
    b = z * (1 - core) + y * core
    stride_a = 1 + 3 * core
    stride_b = 4 - 3 * core

    def device(a_pos, b_pos):
        return {"vocab": (a_pos * stride_a + b_pos * stride_b) * 2 + core}

    def on_y(d):
        return {"vocab": (z * 4 + (y + d) % 4) * 2 + core}

    def on_z(d):
        return {"vocab": (((z + d) % 4) * 4 + y) * 2 + core}

    def remote(src, dst, send, recv, where):
        return pltpu.make_async_remote_copy(src, dst, send, recv, device_id=where, device_id_type=MESH)

    mate = {"vocab": me + 1 - 2 * core}
    a_right, a_left = (a + 1) % 4, (a + 3) % 4
    my_slot = core * 16 + a * 4 + b

    def start(copies):
        for copy in copies:
            copy.start()

    def arrived(copies):
        for copy in copies:
            copy.wait_recv()

    def left(copies):
        for copy in copies:
            copy.wait_send()

    for v in range(NV):
        s = slot_of(v)
        pltpu.make_async_copy(hidden.at[pl.ds(v * OWN, OWN)], h.at[pl.ds(s * OWN, OWN)], h_sem).start()

    def w_copy(n):
        rows = pl.ds(n * 256, 256)
        return pltpu.make_async_copy(weight.at[rows], w.at[rows], w_sem.at[n])

    def w_tail():
        rows = pl.ds(MAIN, TAIL)
        return pltpu.make_async_copy(weight.at[rows], w.at[rows], w_sem.at[NB])

    for n in range(NB):
        w_copy(n).start()
    w_tail().start()

    barrier = pltpu.get_barrier_semaphore()
    for where in [mate] + [on_y(d) for d in (1, 2, 3)] + [on_z(d) for d in (1, 2, 3)]:
        pl.semaphore_signal(barrier, inc=1, device_id=where, device_id_type=MESH)
    tl = tlog_ref[...]
    shifted = tl - jnp.max(tl, axis=1, keepdims=True)
    log_probs = shifted - jnp.log(jnp.sum(jnp.exp(shifted), axis=1, keepdims=True))
    probs = jnp.exp(log_probs)
    negent = jnp.sum(probs * log_probs, axis=1, keepdims=True)
    ids = ids_ref[...].astype(jnp.float32)
    for i in range(2):
        for t in range(8):
            token = slice(i * 8 + t, i * 8 + t + 1)
            comb[z, y, core, i:i + 1, t * K:(t + 1) * K] = ids[token]
            comb[z, y, core, 2 + i:3 + i, t * K:(t + 1) * K] = probs[token]

    def comb_copies(k):
        if k == 0:
            block = comb.at[z, y, core]
            return [remote(block, block, comb_send.at[0], comb_recv.at[0], mate)]
        block = comb.at[z, y] if k == 1 else comb.at[z]
        return [
            remote(block, block, comb_send.at[3 * k - 3 + d], comb_recv.at[3 * k - 3 + d], (on_y if k == 1 else on_z)(d))
            for d in (1, 2, 3)
        ]

    pltpu.make_async_copy(h, h, h_sem).wait()

    def logits_block(n):
        w_copy(n).wait()
        block = pl.ds(pl.multiple_of(n * 256, 256), 256)
        logits[:, block] = lax.dot_general(h[...], w[block, :], NT, preferred_element_type=jnp.float32)

    pl.loop(0, 2)(logits_block)
    pl.semaphore_wait(barrier, 7)
    start(comb_copies(0))
    pl.loop(2, 4)(logits_block)
    arrived(comb_copies(0))
    start(comb_copies(1))
    pl.loop(4, 7)(logits_block)
    arrived(comb_copies(1))
    start(comb_copies(2))
    pl.loop(7, NB)(logits_block)

    w_tail().wait()
    w[COLS:, :] = jnp.zeros((PADDED - COLS, D), jnp.bfloat16)
    logits[:, MAIN:] = lax.dot_general(h[...], w[MAIN:, :], NT, preferred_element_type=jnp.float32)

    lane = lax.broadcasted_iota(jnp.int32, (8, 128), 1)

    @pl.loop(0, TOK // 8, unroll=8)
    def _(i):
        rows = pl.ds(pl.multiple_of(i * 8, 8), 8)
        tiles = [logits[rows, t * 128:(t + 1) * 128] for t in range(TILES)]
        tiles[-1] = jnp.where(lane < TAIL, tiles[-1], jnp.float32(-1e30))
        top = functools.reduce(jnp.maximum, tiles)
        m = jnp.max(top, axis=1, keepdims=True)
        acc = functools.reduce(jnp.add, [jnp.exp(t - m) for t in tiles])
        s = jnp.sum(acc, axis=1, keepdims=True)
        lsecol[rows, :] = jnp.broadcast_to(m + jnp.log(s), (8, 128))

    def original_rows(col, i):
        return jnp.concatenate([col[pl.ds(slot_of(8 * i + j) * OWN, OWN), :] for j in range(8)], axis=0)

    def in_rows(col):
        return jnp.concatenate([jnp.transpose(original_rows(col, i))[0:1, :] for i in range(4)], axis=0)

    def stat_copies(which, k):
        if k == 0:
            block = stat_core.at[which, core]
            return [remote(block, block, st_send.at[which, 0], st_recv.at[which, 0], mate)]
        block = stat_y.at[which, y] if k == 1 else stat_z.at[which, z]
        return [
            remote(block, block, st_send.at[which, 3 * k - 3 + d], st_recv.at[which, 3 * k - 3 + d], (on_y if k == 1 else on_z)(d))
            for d in (1, 2, 3)
        ]

    def log_add(stats):
        top = jnp.max(stats, axis=0)
        return top + jnp.log(jnp.sum(jnp.exp(stats - top[None]), axis=0))

    stat_core[0, core] = in_rows(lsecol)
    start(stat_copies(0, 0))

    arrived(comb_copies(2))
    first = (me * COLS).astype(jnp.float32)
    bf16 = jnp.bfloat16
    row16 = lax.broadcasted_iota(jnp.int32, (16, 256), 0)
    lane256 = lax.broadcasted_iota(jnp.int32, (16, 256), 1)
    same_token = (row16 % 4) == (lane256 // K)
    tile_of_row = [
        (row16 // 4).astype(jnp.float32).astype(bf16),
        ((row16 // 4) ^ 1).astype(jnp.float32).astype(bf16),
    ]
    column_of_row = row16.astype(jnp.float32).astype(bf16)
    zero, one = jnp.zeros((16, 256), bf16), jnp.ones((16, 256), bf16)
    first_four = lax.broadcasted_iota(jnp.int32, (8, 128), 0) < 4

    def wide(row):
        return jnp.broadcast_to(row, (16, 256))

    def target_rows(i):
        rows = pl.ds(pl.multiple_of(i * 8, 8), 8)
        half, slot = i % 2, i // 2
        slot_core, outer, inner = slot // 16, (slot // 4) % 4, slot % 4
        slot_y = outer * (1 - slot_core) + inner * slot_core
        slot_z = inner * (1 - slot_core) + outer * slot_core
        offset = comb[slot_z, slot_y, slot_core, pl.ds(half, 1), :] - first
        inside = (offset >= 0) & (offset < COLS)
        tile = jnp.floor(offset * jnp.float32(1 / 128))
        column = offset - tile * 128
        tile = jnp.where(inside, tile, jnp.float32(-8))
        rest = comb[slot_z, slot_y, slot_core, pl.ds(2 + half, 1), :]
        parts = []
        for _ in range(3):
            parts.append(rest.astype(bf16).astype(jnp.float32))
            rest = rest - parts[-1]
        placed = []
        for k in range(2):
            at = slice(k * 256, (k + 1) * 256)
            tiles = jnp.where(same_token, wide(tile[:, at]), jnp.float32(-8)).astype(bf16) - tile_of_row[k]
            masks = [tiles == bf16(4 * j) for j in range(5)]
            left_side = [jnp.where(m, part, zero) for part in [wide(p[:, at]).astype(bf16) for p in parts] for m in masks]
            columns = wide(column[:, at]).astype(bf16) - column_of_row
            right_side = [jnp.where(columns == bf16(16 * j), one, zero) for j in range(8)]
            out = lax.dot_general(
                jnp.concatenate(left_side, axis=0), jnp.concatenate(right_side, axis=0), NT, preferred_element_type=jnp.float32)
            placed.append(out[0:80] + out[80:160] + out[160:240])
        cross = jnp.zeros((8, 128), jnp.float32)
        for t in range(TILES):
            at, pair = slice(t * 128, (t + 1) * 128), slice(t // 2 * 8, t // 2 * 8 + 8)
            if t % 2 == 0:
                value = jnp.where(first_four, placed[0][pair], placed[1][pair])
            else:
                value = pltpu.roll(jnp.where(first_four, placed[1][pair], placed[0][pair]), 4, 0)
            target[rows, at] = value
            cross = cross + value * logits[rows, at]
        crosscol[rows, :] = jnp.broadcast_to(jnp.sum(cross, axis=1, keepdims=True), (8, 128))

    pl.loop(0, 16, unroll=8)(target_rows)
    arrived(stat_copies(0, 0))
    stat_y[0, y] = log_add(stat_core[0])
    start(stat_copies(0, 1))
    pl.loop(16, 40, unroll=8)(target_rows)
    arrived(stat_copies(0, 1))
    stat_z[0, z] = log_add(stat_y[0])
    start(stat_copies(0, 2))
    pl.loop(40, 64, unroll=8)(target_rows)
    own_rows = pl.ds(pl.multiple_of(my_slot * OWN, OWN), OWN)
    crosscol[own_rows, :] = crosscol[own_rows, :] - negent
    arrived(stat_copies(0, 2))
    log_total = log_add(stat_z[0])
    for i in range(4):
        col = jnp.transpose(jnp.broadcast_to(log_total[i:i + 1, :], (128, 128)))
        for j in range(8):
            ltcol[pl.ds(slot_of(8 * i + j) * OWN, OWN), :] = col[j * OWN:(j + 1) * OWN, :]

    lane16 = lax.broadcasted_iota(jnp.int32, (16, 128), 1)

    @pl.loop(0, TOK // 16)
    def _(i):
        rows = pl.ds(pl.multiple_of(i * 16, 16), 16)
        lt = ltcol[rows, :]
        for t in range(TILES):
            at = slice(t * 128, (t + 1) * 128)
            value = jnp.exp(logits[rows, at] - lt) - target[rows, at]
            if t == TILES - 1:
                value = jnp.where(lane16 < TAIL, value, jnp.float32(0.0))
            gm[rows, at] = value.astype(jnp.bfloat16)

    def multiply(unit):
        c = max(k for k in range(NC) if sum(CHUNKS[:k]) <= unit)
        at = (unit - sum(CHUNKS[:c])) * UNIT
        part = jnp.dot(gm[...], w[:, unit * UNIT:(unit + 1) * UNIT], preferred_element_type=jnp.float32)
        g[c][:, :, :, :, at:at + UNIT] = part.reshape(2, 4, 4, OWN, UNIT)

    def step_core(c):
        return [remote(g[c].at[1 - core], cr[c], g_send.at[c, 0], g_recv.at[c, 0], mate)]

    def step_far(c):
        far = (a + 2) % 4
        return [
            remote(g[c].at[core, far, 0:2], r11[c].at[0], g_send.at[c, 1], g_recv.at[c, 1], device(a_right, b)),
            remote(g[c].at[core, far, 2:4], r11[c].at[1], g_send.at[c, 2], g_recv.at[c, 2], device(a_left, b)),
        ]

    def step_near(c):
        return [
            remote(g[c].at[core, a_right], r12[c].at[0], g_send.at[c, 3], g_recv.at[c, 3], device(a_right, b)),
            remote(g[c].at[core, a_left], r12[c].at[1], g_send.at[c, 4], g_recv.at[c, 4], device(a_left, b)),
        ]

    def step_last(c):
        return [
            remote(g[c].at[core, a, (b + d) % 4], r2[c].at[d - 1], g_send.at[c, 4 + d], g_recv.at[c, 4 + d], device(a, (b + d) % 4))
            for d in (1, 2, 3)
        ]

    unit = 0
    for event in ORDER:
        if event == "m":
            multiply(unit)
            unit += 1
            continue
        kind, c = event[0], int(event[1])
        if kind == "C":
            start(step_core(c))
        elif kind == "X":
            arrived(step_core(c))
            for k in range(4):
                g[c][core, k] = g[c][core, k] + cr[c][k]
            start(step_far(c))
        elif kind == "Y":
            arrived(step_far(c))
            g[c][core, a_right, 0:2] = g[c][core, a_right, 0:2] + r11[c][0]
            g[c][core, a_left, 2:4] = g[c][core, a_left, 2:4] + r11[c][1]
            start(step_near(c))
        elif kind == "Z":
            arrived(step_near(c))
            g[c][core, a] = g[c][core, a] + (r12[c][0] + r12[c][1])
            start(step_last(c))
        elif kind == "F":
            arrived(step_last(c))
            at = sum(CHUNKS[:c]) * UNIT
            grad_out[:, at:at + CHUNKS[c] * UNIT] = g[c][core, a, b] + ((r2[c][0] + r2[c][1]) + r2[c][2])
        elif c == 1:
            stat_core[1, core] = in_rows(crosscol)
            start(stat_copies(1, 0))
        elif c == 2:
            arrived(stat_copies(1, 0))
            stat_y[1, y] = jnp.sum(stat_core[1], axis=0)
            start(stat_copies(1, 1))
        elif c == 3:
            arrived(stat_copies(1, 1))
            stat_z[1, z] = jnp.sum(stat_y[1], axis=0)
            start(stat_copies(1, 2))
        else:
            arrived(stat_copies(1, 2))
            loss_out[...] = log_total - jnp.sum(stat_z[1], axis=0)

    for k in range(3):
        left(comb_copies(k) + stat_copies(0, k) + stat_copies(1, k))
    for c in range(NC):
        left(step_core(c) + step_far(c) + step_near(c) + step_last(c))


def local(hidden, head_weight, teacher_ids, teacher_logits):
    any_space = pl.BlockSpec(memory_space=pl.ANY)
    vmem = pl.BlockSpec(memory_space=pltpu.VMEM)
    f32, bf16 = jnp.float32, jnp.bfloat16
    dma = pltpu.SemaphoreType.DMA
    widths = [k * UNIT for k in CHUNKS]
    grad, loss = pl.pallas_call(
        kernel,
        out_shape=(jax.ShapeDtypeStruct((OWN, D), f32), jax.ShapeDtypeStruct((4, 128), f32)),
        in_specs=[any_space, any_space, vmem, vmem],
        out_specs=(vmem, vmem),
        scratch_shapes=[
            pltpu.VMEM((PADDED, D), bf16),
            pltpu.VMEM((TOK, D), bf16),
            pltpu.VMEM((TOK, PADDED), f32),
            pltpu.VMEM((TOK, PADDED), f32),
            pltpu.VMEM((TOK, PADDED), bf16),
            [pltpu.VMEM((2, 4, 4, OWN, k), f32) for k in widths],
            [pltpu.VMEM((4, 4, OWN, k), f32) for k in widths],
            [pltpu.VMEM((2, 2, OWN, k), f32) for k in widths],
            [pltpu.VMEM((2, 4, OWN, k), f32) for k in widths],
            [pltpu.VMEM((3, OWN, k), f32) for k in widths],
            pltpu.VMEM((4, 4, 2, 4, 8 * K), f32),
            pltpu.VMEM((2, 2, 4, 128), f32),
            pltpu.VMEM((2, 4, 4, 128), f32),
            pltpu.VMEM((2, 4, 4, 128), f32),
            pltpu.VMEM((TOK, 128), f32),
            pltpu.VMEM((TOK, 128), f32),
            pltpu.VMEM((TOK, 128), f32),
            dma, dma((NB + 1,)), dma((7,)), dma((7,)), dma((2, 7)), dma((2, 7)), dma((NC, 8)), dma((NC, 8)),
        ],
        compiler_params=pltpu.CompilerParams(
            collective_id=0, has_side_effects=True, vmem_limit_bytes=60 * 1024 * 1024),
    )(hidden, head_weight.T, teacher_ids, teacher_logits)
    return loss.reshape(TOK), grad


def solution(mesh):
    placed = (P("dp", None), P(None, "vocab"), P(("dp", "vocab"), None), P(("dp", "vocab"), None))
    return jax.shard_map(
        local,
        mesh=mesh,
        in_specs=placed,
        out_specs=(P("dp"), P(("dp", "vocab"), None)),
        check_vma=False,
    )
```

```python
import functools

import jax
import jax.numpy as jnp
from jax import lax
from jax.experimental import pallas as pl
from jax.experimental.pallas import tpu as pltpu
from jax.sharding import PartitionSpec as P

MESH = pl.DeviceIdType.MESH
NV = 32
TOK = 512
OWN = 16
D = 3584
COLS = 2376
MAIN = 2304
TAIL = COLS - MAIN
PADDED = MAIN + 128
TILES = PADDED // 128
NB = MAIN // 256
UNIT = 256
CHUNKS = (1, 2, 3, 3, 3, 2)
NC = len(CHUNKS)
STRAIGHT = (4, 5)
K = 64
ORDER = (
    "m", "m", "m", "C1", "C0", "m", "m", "X1", "m", "C2", "X0", "m", "m", "X2", "m", "C3", "Y1",
    "m", "Y0", "m", "X3", "m", "C4", "Y2", "m", "m", "X4", "C5", "Y3", "K1", "Z2", "X5", "Z0", "Y4",
    "Z3", "Y5", "Z1", "W0", "W2", "Z4", "W3", "Z5", "W1", "K2", "F4", "F3", "F2", "F0", "F5", "K3",
    "F1",
)
NT = (((1,), (1,)), ((), ()))


def slot_of(index):
    core, y, z = index % 2, (index // 2) % 4, index // 8
    return core * 16 + (y * 4 + z) * (1 - core) + (z * 4 + y) * core


def kernel(
    hidden, weight, ids_ref, tlog_ref,
    grad_out, loss_out,
    w, h, logits, target, gm, g, cr, r11, r12, r2,
    comb, stat_core, stat_chip, ltcol, top, total, cross,
    h_sem, w_sem, comb_send, comb_recv, st_send, st_recv, g_send, g_recv,
):
    me = lax.axis_index("vocab")
    core = me % 2
    y = (me // 2) % 4
    z = me // 8
    a = y * (1 - core) + z * core
    b = z * (1 - core) + y * core
    stride_a = 1 + 3 * core
    stride_b = 4 - 3 * core

    def device(a_pos, b_pos):
        return {"vocab": (a_pos * stride_a + b_pos * stride_b) * 2 + core}

    def chip(dy, dz):
        return {"vocab": (((z + dz) % 4) * 4 + (y + dy) % 4) * 2 + core}

    others = [(dy, dz) for dz in range(4) for dy in range(4) if dy or dz]

    def remote(src, dst, send, recv, where):
        return pltpu.make_async_remote_copy(src, dst, send, recv, device_id=where, device_id_type=MESH)

    mate = {"vocab": me + 1 - 2 * core}
    a_right, a_left = (a + 1) % 4, (a + 3) % 4
    b_right, b_left = (b + 1) % 4, (b + 3) % 4
    my_slot = core * 16 + a * 4 + b

    def start(copies):
        for copy in copies:
            copy.start()

    def arrived(copies):
        for copy in copies:
            copy.wait_recv()

    def left(copies):
        for copy in copies:
            copy.wait_send()

    for v in range(NV):
        s = slot_of(v)
        pltpu.make_async_copy(hidden.at[pl.ds(v * OWN, OWN)], h.at[pl.ds(s * OWN, OWN)], h_sem).start()

    def w_copy(n):
        rows = pl.ds(n * 256, 256)
        return pltpu.make_async_copy(weight.at[rows], w.at[rows], w_sem.at[n])

    def w_tail():
        rows = pl.ds(MAIN, TAIL)
        return pltpu.make_async_copy(weight.at[rows], w.at[rows], w_sem.at[NB])

    for n in range(NB):
        w_copy(n).start()
    w_tail().start()

    barrier = pltpu.get_barrier_semaphore()
    for where in [mate] + [chip(dy, dz) for dy, dz in others]:
        pl.semaphore_signal(barrier, inc=1, device_id=where, device_id_type=MESH)
    tl = tlog_ref[...]
    shifted = tl - jnp.max(tl, axis=1, keepdims=True)
    log_probs = shifted - jnp.log(jnp.sum(jnp.exp(shifted), axis=1, keepdims=True))
    probs = jnp.exp(log_probs)
    negent = jnp.sum(probs * log_probs, axis=1, keepdims=True)
    ids = ids_ref[...].astype(jnp.float32)
    for i in range(2):
        for t in range(8):
            token = slice(i * 8 + t, i * 8 + t + 1)
            comb[core, z, y, i:i + 1, t * K:(t + 1) * K] = ids[token]
            comb[core, z, y, 2 + i:3 + i, t * K:(t + 1) * K] = probs[token]

    def comb_copies(k):
        if k == 1:
            return [remote(comb.at[core], comb.at[core], comb_send.at[15], comb_recv.at[15], mate)]
        block = comb.at[core, z, y]
        return [
            remote(block, block, comb_send.at[i], comb_recv.at[i], chip(dy, dz)) for i, (dy, dz) in enumerate(others)
        ]

    def stat_copies(which, k):
        if k == 0:
            block = stat_core.at[which, core]
            return [remote(block, block, st_send.at[which, 15], st_recv.at[which, 15], mate)]
        block = stat_chip.at[which, z * 4 + y]
        return [
            remote(block, block, st_send.at[which, i], st_recv.at[which, i], chip(dy, dz))
            for i, (dy, dz) in enumerate(others)
        ]

    def log_add(stats):
        peak = jnp.max(stats, axis=0)
        return peak + jnp.log(jnp.sum(jnp.exp(stats - peak[None]), axis=0))

    first = (me * COLS).astype(jnp.float32)
    bf16 = jnp.bfloat16
    row16 = lax.broadcasted_iota(jnp.int32, (16, 256), 0)
    lane256 = lax.broadcasted_iota(jnp.int32, (16, 256), 1)
    same_token = (row16 % 4) == (lane256 // K)
    tile_of_row = [
        (row16 // 4).astype(jnp.float32).astype(bf16),
        ((row16 // 4) ^ 1).astype(jnp.float32).astype(bf16),
    ]
    column_of_row = row16.astype(jnp.float32).astype(bf16)
    zero, one = jnp.zeros((16, 256), bf16), jnp.ones((16, 256), bf16)
    first_four = lax.broadcasted_iota(jnp.int32, (8, 128), 0) < 4

    def wide(row):
        return jnp.broadcast_to(row, (16, 256))

    def target_rows(i):
        rows = pl.ds(pl.multiple_of(i * 8, 8), 8)
        half, slot = i % 2, i // 2
        slot_core, outer, inner = slot // 16, (slot // 4) % 4, slot % 4
        slot_y = outer * (1 - slot_core) + inner * slot_core
        slot_z = inner * (1 - slot_core) + outer * slot_core
        offset = comb[slot_core, slot_z, slot_y, pl.ds(half, 1), :] - first
        inside = (offset >= 0) & (offset < COLS)
        tile = jnp.floor(offset * jnp.float32(1 / 128))
        column = offset - tile * 128
        tile = jnp.where(inside, tile, jnp.float32(-8))
        rest = comb[slot_core, slot_z, slot_y, pl.ds(2 + half, 1), :]
        parts = []
        for _ in range(3):
            parts.append(rest.astype(bf16).astype(jnp.float32))
            rest = rest - parts[-1]
        placed = []
        for k in range(2):
            at = slice(k * 256, (k + 1) * 256)
            tiles = jnp.where(same_token, wide(tile[:, at]), jnp.float32(-8)).astype(bf16) - tile_of_row[k]
            masks = [tiles == bf16(4 * j) for j in range(5)]
            left_side = [jnp.where(m, part, zero) for part in [wide(p[:, at]).astype(bf16) for p in parts] for m in masks]
            columns = wide(column[:, at]).astype(bf16) - column_of_row
            right_side = [jnp.where(columns == bf16(16 * j), one, zero) for j in range(8)]
            out = lax.dot_general(
                jnp.concatenate(left_side, axis=0), jnp.concatenate(right_side, axis=0), NT, preferred_element_type=jnp.float32)
            placed.append(out[0:80] + out[80:160] + out[160:240])
        for t in range(TILES):
            at, pair = slice(t * 128, (t + 1) * 128), slice(t // 2 * 8, t // 2 * 8 + 8)
            if t % 2 == 0:
                value = jnp.where(first_four, placed[0][pair], placed[1][pair])
            else:
                value = pltpu.roll(jnp.where(first_four, placed[1][pair], placed[0][pair]), 4, 0)
            target[rows, at] = value

    lane = lax.broadcasted_iota(jnp.int32, (16, 128), 1)

    def running(n, last=False):
        for r in range(0, TOK, 16):
            rows = slice(r, r + 16)
            values = [logits[rows, pl.ds(n * 256 if isinstance(n, int) else pl.multiple_of(n * 256, 256), 128)]]
            if last:
                values = [jnp.where(lane < TAIL, values[0], jnp.float32(-1e30))]
            else:
                at = n * 256 + 128
                values.append(logits[rows, pl.ds(at if isinstance(n, int) else pl.multiple_of(at, 128), 128)])
            peak = functools.reduce(jnp.maximum, values)
            old = top[rows, :]
            peak = jnp.maximum(old, peak)
            sums = functools.reduce(jnp.add, [jnp.exp(v - peak) for v in values])
            sums = sums + total[rows, :] * jnp.exp(old - peak)
            top[rows, :] = peak
            total[rows, :] = sums

    def logits_block(n, size):
        block = pl.ds(n * 256 if isinstance(n, int) else pl.multiple_of(n * 256, 256), size)
        logits[:, block] = lax.dot_general(h[...], w[block, :], NT, preferred_element_type=jnp.float32)

    def pairs(low, high, whole=True):
        @pl.loop(low, high)
        def _(k):
            w_copy(2 * k - 1).wait()
            w_copy(2 * k).wait()
            if whole:
                running(2 * k - 3)
            running(2 * k - 2)
            logits_block(2 * k - 1, 512)

    pltpu.make_async_copy(h, h, h_sem).wait()
    w_copy(0).wait()
    logits_block(0, 256)
    top[...] = jnp.full((TOK, 128), -1e30, jnp.float32)
    total[...] = jnp.zeros((TOK, 128), jnp.float32)
    pl.semaphore_wait(barrier, 16)
    start(comb_copies(0))
    pairs(1, 2, whole=False)
    pairs(2, 3)
    arrived(comb_copies(0))
    start(comb_copies(1))
    pairs(3, (NB + 1) // 2)
    w_tail().wait()
    w[COLS:, :] = jnp.zeros((PADDED - COLS, D), jnp.bfloat16)
    running(NB - 2)
    running(NB - 1)
    logits[:, MAIN:] = lax.dot_general(h[...], w[MAIN:, :], NT, preferred_element_type=jnp.float32)
    running(NB, last=True)

    def original_rows(col, i):
        return jnp.concatenate([col[pl.ds(slot_of(8 * i + j) * OWN, OWN), :] for j in range(8)], axis=0)

    def lse_rows(i):
        peaks, sums = jnp.transpose(original_rows(top, i)), jnp.transpose(original_rows(total, i))
        peak = jnp.max(peaks, axis=0, keepdims=True)
        return peak + jnp.log(jnp.sum(sums * jnp.exp(peaks - peak), axis=0, keepdims=True))

    stat_core[0, core] = jnp.concatenate([lse_rows(i) for i in range(4)], axis=0)
    start(stat_copies(0, 0))

    arrived(comb_copies(1))
    pl.loop(0, 16, unroll=8)(target_rows)
    arrived(stat_copies(0, 0))
    stat_chip[0, z * 4 + y] = log_add(stat_core[0])
    start(stat_copies(0, 1))
    pl.loop(16, TOK // 8, unroll=8)(target_rows)
    arrived(stat_copies(0, 1))
    log_total = log_add(stat_chip[0])
    for i in range(4):
        col = jnp.transpose(jnp.broadcast_to(log_total[i:i + 1, :], (128, 128)))
        for j in range(8):
            ltcol[pl.ds(slot_of(8 * i + j) * OWN, OWN), :] = col[j * OWN:(j + 1) * OWN, :]

    @pl.loop(0, TOK // 16, unroll=2)
    def _(i):
        rows = pl.ds(pl.multiple_of(i * 16, 16), 16)
        lt = ltcol[rows, :]
        terms = jnp.zeros((16, 128), jnp.float32)
        for t in range(TILES):
            at = slice(t * 128, (t + 1) * 128)
            logit, want = logits[rows, at], target[rows, at]
            terms = terms + want * logit
            value = jnp.exp(logit - lt) - want
            if t == TILES - 1:
                value = jnp.where(lane < TAIL, value, jnp.float32(0.0))
            gm[rows, at] = value.astype(jnp.bfloat16)
        cross[rows, :] = terms

    own_rows = pl.ds(pl.multiple_of(my_slot * OWN, OWN), OWN)
    cross[own_rows, :] = cross[own_rows, :] - jnp.where(lane == 0, negent, jnp.float32(0.0))

    def multiply(unit):
        c = max(k for k in range(NC) if sum(CHUNKS[:k]) <= unit)
        at = (unit - sum(CHUNKS[:c])) * UNIT
        part = jnp.dot(gm[...], w[:, unit * UNIT:(unit + 1) * UNIT], preferred_element_type=jnp.float32)
        g[c][:, :, :, :, at:at + UNIT] = part.reshape(2, 4, 4, OWN, UNIT)

    def step_core(c):
        return [remote(g[c].at[1 - core], cr[c], g_send.at[c, 0], g_recv.at[c, 0], mate)]

    def step_far(c):
        far = (a + 2) % 4
        return [
            remote(g[c].at[core, far, 0:2], r11[c].at[0], g_send.at[c, 1], g_recv.at[c, 1], device(a_right, b)),
            remote(g[c].at[core, far, 2:4], r11[c].at[1], g_send.at[c, 2], g_recv.at[c, 2], device(a_left, b)),
        ]

    def step_near(c):
        return [
            remote(g[c].at[core, a_right], r12[c].at[0], g_send.at[c, 3], g_recv.at[c, 3], device(a_right, b)),
            remote(g[c].at[core, a_left], r12[c].at[1], g_send.at[c, 4], g_recv.at[c, 4], device(a_left, b)),
        ]

    def step_far2(c):
        if c in STRAIGHT:
            return [
                remote(g[c].at[core, a, (b + d) % 4], r2[c].at[d - 1], g_send.at[c, 4 + d], g_recv.at[c, 4 + d], device(a, (b + d) % 4))
                for d in (1, 2, 3)
            ]
        far = (b + 2) % 4
        return [
            remote(g[c].at[core, a, far, 0:8], r2[c].at[2, 0:8], g_send.at[c, 5], g_recv.at[c, 5], device(a, b_right)),
            remote(g[c].at[core, a, far, 8:16], r2[c].at[2, 8:16], g_send.at[c, 6], g_recv.at[c, 6], device(a, b_left)),
        ]

    def step_near2(c):
        return [
            remote(g[c].at[core, a, b_right], r2[c].at[0], g_send.at[c, 7], g_recv.at[c, 7], device(a, b_right)),
            remote(g[c].at[core, a, b_left], r2[c].at[1], g_send.at[c, 8], g_recv.at[c, 8], device(a, b_left)),
        ]

    unit = 0
    for event in ORDER:
        if event == "m":
            multiply(unit)
            unit += 1
            continue
        kind, c = event[0], int(event[1])
        if kind == "C":
            start(step_core(c))
        elif kind == "X":
            arrived(step_core(c))
            for k in range(4):
                g[c][core, k] = g[c][core, k] + cr[c][k]
            start(step_far(c))
        elif kind == "Y":
            arrived(step_far(c))
            g[c][core, a_right, 0:2] = g[c][core, a_right, 0:2] + r11[c][0]
            g[c][core, a_left, 2:4] = g[c][core, a_left, 2:4] + r11[c][1]
            start(step_near(c))
        elif kind == "Z":
            arrived(step_near(c))
            g[c][core, a] = g[c][core, a] + (r12[c][0] + r12[c][1])
            start(step_far2(c))
        elif kind == "W":
            arrived(step_far2(c))
            g[c][core, a, b_right, 0:8] = g[c][core, a, b_right, 0:8] + r2[c][2, 0:8]
            g[c][core, a, b_left, 8:16] = g[c][core, a, b_left, 8:16] + r2[c][2, 8:16]
            start(step_near2(c))
        elif kind == "F":
            arrived(step_far2(c) if c in STRAIGHT else step_near2(c))
            at = sum(CHUNKS[:c]) * UNIT
            value = g[c][core, a, b] + (r2[c][0] + r2[c][1])
            if c in STRAIGHT:
                value = value + r2[c][2]
            grad_out[:, at:at + CHUNKS[c] * UNIT] = value
        elif c == 1:
            rows = [jnp.sum(jnp.transpose(original_rows(cross, i)), axis=0, keepdims=True) for i in range(4)]
            stat_core[1, core] = jnp.concatenate(rows, axis=0)
            start(stat_copies(1, 0))
        elif c == 2:
            arrived(stat_copies(1, 0))
            stat_chip[1, z * 4 + y] = jnp.sum(stat_core[1], axis=0)
            start(stat_copies(1, 1))
        else:
            arrived(stat_copies(1, 1))
            loss_out[...] = log_total - jnp.sum(stat_chip[1], axis=0)

    for k in range(2):
        left(comb_copies(k) + stat_copies(0, k) + stat_copies(1, k))
    for c in range(NC):
        left(step_core(c) + step_far(c) + step_near(c) + step_far2(c) + ([] if c in STRAIGHT else step_near2(c)))


def finish(grad_ref, loss_ref, grad_out, loss_out):
    grad_out[...] = grad_ref[...]
    loss_out[...] = loss_ref[...]


def local(hidden, head_weight, teacher_ids, teacher_logits):
    any_space = pl.BlockSpec(memory_space=pl.ANY)
    vmem = pl.BlockSpec(memory_space=pltpu.VMEM)
    f32, bf16 = jnp.float32, jnp.bfloat16
    dma = pltpu.SemaphoreType.DMA
    widths = [k * UNIT for k in CHUNKS]
    grad, loss = pl.pallas_call(
        kernel,
        out_shape=(jax.ShapeDtypeStruct((OWN, D), f32), jax.ShapeDtypeStruct((4, 128), f32)),
        in_specs=[any_space, any_space, vmem, vmem],
        out_specs=(vmem, vmem),
        scratch_shapes=[
            pltpu.VMEM((PADDED, D), bf16),
            pltpu.VMEM((TOK, D), bf16),
            pltpu.VMEM((TOK, PADDED), f32),
            pltpu.VMEM((TOK, PADDED), f32),
            pltpu.VMEM((TOK, PADDED), bf16),
            [pltpu.VMEM((2, 4, 4, OWN, k), f32) for k in widths],
            [pltpu.VMEM((4, 4, OWN, k), f32) for k in widths],
            [pltpu.VMEM((2, 2, OWN, k), f32) for k in widths],
            [pltpu.VMEM((2, 4, OWN, k), f32) for k in widths],
            [pltpu.VMEM((3, OWN, k), f32) for k in widths],
            pltpu.VMEM((2, 4, 4, 4, 8 * K), f32),
            pltpu.VMEM((2, 2, 4, 128), f32),
            pltpu.VMEM((2, 16, 4, 128), f32),
            pltpu.VMEM((TOK, 128), f32),
            pltpu.VMEM((TOK, 128), f32),
            pltpu.VMEM((TOK, 128), f32),
            pltpu.VMEM((TOK, 128), f32),
            dma, dma((NB + 1,)), dma((16,)), dma((16,)), dma((2, 16)), dma((2, 16)), dma((NC, 9)), dma((NC, 9)),
        ],
        compiler_params=pltpu.CompilerParams(
            collective_id=0, has_side_effects=True, vmem_limit_bytes=60 * 1024 * 1024),
    )(hidden, head_weight.T, teacher_ids, teacher_logits)
    grad, loss = pl.pallas_call(
        finish,
        out_shape=(jax.ShapeDtypeStruct((OWN, D), f32), jax.ShapeDtypeStruct((4, 128), f32)),
        in_specs=[vmem, vmem],
        out_specs=(vmem, vmem),
    )(grad, loss)
    return loss.reshape(TOK), grad


def solution(mesh):
    placed = (P("dp", None), P(None, "vocab"), P(("dp", "vocab"), None), P(("dp", "vocab"), None))
    return jax.shard_map(
        local,
        mesh=mesh,
        in_specs=placed,
        out_specs=(P("dp"), P(("dp", "vocab"), None)),
        check_vma=False,
    )
```

```python
import functools

import jax
import jax.numpy as jnp
from jax import lax
from jax.experimental import pallas as pl
from jax.experimental.pallas import tpu as pltpu
from jax.sharding import PartitionSpec as P

MESH = pl.DeviceIdType.MESH
NV = 32
TOK = 512
OWN = 16
D = 3584
COLS = 2376
MAIN = 2304
TAIL = COLS - MAIN
PADDED = MAIN + 128
TILES = PADDED // 128
NB = MAIN // 256
UNIT = 256
CHUNKS = (3, 4, 4, 3)
NC = len(CHUNKS)
STRAIGHT = (2, 3)
K = 64
ORDER = (
    "m", "m", "m", "C0", "m", "m", "X0", "m", "m", "C1", "m", "m", "X1", "Y0", "m", "m", "C2", "m",
    "m", "X2", "Y1", "m", "C3", "X3", "Y2", "K1", "Z0", "Y3", "Z1", "K2", "Z2", "W0", "Z3", "W1",
    "K3", "F0", "F1", "F2", "F3",
)
NT = (((1,), (1,)), ((), ()))


def slot_of(index):
    core, y, z = index % 2, (index // 2) % 4, index // 8
    return core * 16 + (y * 4 + z) * (1 - core) + (z * 4 + y) * core


def kernel(
    hidden, weight, ids_hbm, tlog_hbm,
    grad_out, loss_out,
    w, h, logits, target, gm, g, cr, r11, r12, r2,
    comb, stat_core, stat_chip, ltcol, top, total, cross,
    ids_ref, tlog_ref, t_sem, h_sem, w_sem, comb_send, comb_recv, st_send, st_recv, g_send, g_recv,
):
    me = lax.axis_index("vocab")
    core = me % 2
    y = (me // 2) % 4
    z = me // 8
    a = y * (1 - core) + z * core
    b = z * (1 - core) + y * core
    stride_a = 1 + 3 * core
    stride_b = 4 - 3 * core

    def device(a_pos, b_pos):
        return {"vocab": (a_pos * stride_a + b_pos * stride_b) * 2 + core}

    def chip(dy, dz):
        return {"vocab": (((z + dz) % 4) * 4 + (y + dy) % 4) * 2 + core}

    others = [(dy, dz) for dz in range(4) for dy in range(4) if dy or dz]

    def remote(src, dst, send, recv, where):
        return pltpu.make_async_remote_copy(src, dst, send, recv, device_id=where, device_id_type=MESH)

    mate = {"vocab": me + 1 - 2 * core}
    a_right, a_left = (a + 1) % 4, (a + 3) % 4
    b_right, b_left = (b + 1) % 4, (b + 3) % 4
    my_slot = core * 16 + a * 4 + b

    def start(copies):
        for copy in copies:
            copy.start()

    def arrived(copies):
        for copy in copies:
            copy.wait_recv()

    def left(copies):
        for copy in copies:
            copy.wait_send()

    def w_copy(n):
        rows = pl.ds(n * 256, 256)
        return pltpu.make_async_copy(weight.at[rows], w.at[rows], w_sem.at[n])

    def w_tail():
        rows = pl.ds(MAIN, TAIL)
        return pltpu.make_async_copy(weight.at[rows], w.at[rows], w_sem.at[NB])

    teacher = [
        pltpu.make_async_copy(ids_hbm, ids_ref, t_sem.at[0]),
        pltpu.make_async_copy(tlog_hbm, tlog_ref, t_sem.at[1]),
    ]
    start(teacher)
    w_copy(0).start()
    for k in range(4):
        pltpu.make_async_copy(hidden.at[:, k, 0], h.at[0, k], h_sem).start()
        pltpu.make_async_copy(hidden.at[k, :, 1], h.at[1, k], h_sem).start()
    for n in range(1, NB):
        w_copy(n).start()
    w_tail().start()

    barrier = pltpu.get_barrier_semaphore()
    for where in [mate] + [chip(dy, dz) for dy, dz in others]:
        pl.semaphore_signal(barrier, inc=1, device_id=where, device_id_type=MESH)
    for copy in teacher:
        copy.wait()
    tl = tlog_ref[...]
    shifted = tl - jnp.max(tl, axis=1, keepdims=True)
    log_probs = shifted - jnp.log(jnp.sum(jnp.exp(shifted), axis=1, keepdims=True))
    probs = jnp.exp(log_probs)
    negent = jnp.sum(probs * log_probs, axis=1, keepdims=True)
    ids = ids_ref[...].astype(jnp.float32)
    for i in range(2):
        for t in range(8):
            token = slice(i * 8 + t, i * 8 + t + 1)
            comb[core, z, y, i:i + 1, t * K:(t + 1) * K] = ids[token]
            comb[core, z, y, 2 + i:3 + i, t * K:(t + 1) * K] = probs[token]

    def comb_copies(k):
        if k == 1:
            return [remote(comb.at[core], comb.at[core], comb_send.at[15], comb_recv.at[15], mate)]
        block = comb.at[core, z, y]
        return [
            remote(block, block, comb_send.at[i], comb_recv.at[i], chip(dy, dz)) for i, (dy, dz) in enumerate(others)
        ]

    def stat_copies(which, k):
        if k == 0:
            block = stat_core.at[which, core]
            return [remote(block, block, st_send.at[which, 15], st_recv.at[which, 15], mate)]
        block = stat_chip.at[which, z * 4 + y]
        return [
            remote(block, block, st_send.at[which, i], st_recv.at[which, i], chip(dy, dz))
            for i, (dy, dz) in enumerate(others)
        ]

    def log_add(stats):
        peak = jnp.max(stats, axis=0)
        return peak + jnp.log(jnp.sum(jnp.exp(stats - peak[None]), axis=0))

    first = (me * COLS).astype(jnp.float32)
    bf16 = jnp.bfloat16
    row16 = lax.broadcasted_iota(jnp.int32, (16, 256), 0)
    lane256 = lax.broadcasted_iota(jnp.int32, (16, 256), 1)
    same_token = (row16 % 4) == (lane256 // K)
    tile_of_row = [
        (row16 // 4).astype(jnp.float32).astype(bf16),
        ((row16 // 4) ^ 1).astype(jnp.float32).astype(bf16),
    ]
    column_of_row = row16.astype(jnp.float32).astype(bf16)
    zero, one = jnp.zeros((16, 256), bf16), jnp.ones((16, 256), bf16)
    first_four = lax.broadcasted_iota(jnp.int32, (8, 128), 0) < 4

    def wide(row):
        return jnp.broadcast_to(row, (16, 256))

    def target_rows(i):
        rows = pl.ds(pl.multiple_of(i * 8, 8), 8)
        half, slot = i % 2, i // 2
        slot_core, outer, inner = slot // 16, (slot // 4) % 4, slot % 4
        slot_y = outer * (1 - slot_core) + inner * slot_core
        slot_z = inner * (1 - slot_core) + outer * slot_core
        offset = comb[slot_core, slot_z, slot_y, pl.ds(half, 1), :] - first
        inside = (offset >= 0) & (offset < COLS)
        tile = jnp.floor(offset * jnp.float32(1 / 128))
        column = offset - tile * 128
        tile = jnp.where(inside, tile, jnp.float32(-8))
        rest = comb[slot_core, slot_z, slot_y, pl.ds(2 + half, 1), :]
        parts = []
        for _ in range(3):
            parts.append(rest.astype(bf16).astype(jnp.float32))
            rest = rest - parts[-1]
        placed = []
        for k in range(2):
            at = slice(k * 256, (k + 1) * 256)
            tiles = jnp.where(same_token, wide(tile[:, at]), jnp.float32(-8)).astype(bf16) - tile_of_row[k]
            masks = [tiles == bf16(4 * j) for j in range(5)]
            left_side = [jnp.where(m, part, zero) for part in [wide(p[:, at]).astype(bf16) for p in parts] for m in masks]
            columns = wide(column[:, at]).astype(bf16) - column_of_row
            right_side = [jnp.where(columns == bf16(16 * j), one, zero) for j in range(8)]
            out = lax.dot_general(
                jnp.concatenate(left_side, axis=0), jnp.concatenate(right_side, axis=0), NT, preferred_element_type=jnp.float32)
            placed.append(out[0:80] + out[80:160] + out[160:240])
        for t in range(TILES):
            at, pair = slice(t * 128, (t + 1) * 128), slice(t // 2 * 8, t // 2 * 8 + 8)
            if t % 2 == 0:
                value = jnp.where(first_four, placed[0][pair], placed[1][pair])
            else:
                value = pltpu.roll(jnp.where(first_four, placed[1][pair], placed[0][pair]), 4, 0)
            target[rows, at] = value

    lane = lax.broadcasted_iota(jnp.int32, (16, 128), 1)

    def running(n, last=False):
        for r in range(0, TOK, 16):
            rows = slice(r, r + 16)
            values = [logits[rows, pl.ds(n * 256 if isinstance(n, int) else pl.multiple_of(n * 256, 256), 128)]]
            if last:
                values = [jnp.where(lane < TAIL, values[0], jnp.float32(-1e30))]
            else:
                at = n * 256 + 128
                values.append(logits[rows, pl.ds(at if isinstance(n, int) else pl.multiple_of(at, 128), 128)])
            peak = functools.reduce(jnp.maximum, values)
            old = top[rows, :]
            peak = jnp.maximum(old, peak)
            sums = functools.reduce(jnp.add, [jnp.exp(v - peak) for v in values])
            sums = sums + total[rows, :] * jnp.exp(old - peak)
            top[rows, :] = peak
            total[rows, :] = sums

    def logits_block(n, size):
        block = pl.ds(n * 256 if isinstance(n, int) else pl.multiple_of(n * 256, 256), size)
        logits[:, block] = lax.dot_general(h[...].reshape(TOK, D), w[block, :], NT, preferred_element_type=jnp.float32)

    def pairs(low, high, whole=True):
        @pl.loop(low, high)
        def _(k):
            w_copy(2 * k - 1).wait()
            w_copy(2 * k).wait()
            if whole:
                running(2 * k - 3)
            running(2 * k - 2)
            logits_block(2 * k - 1, 512)

    pltpu.make_async_copy(h, h, h_sem).wait()
    w_copy(0).wait()
    logits_block(0, 256)
    top[...] = jnp.full((TOK, 128), -1e30, jnp.float32)
    total[...] = jnp.zeros((TOK, 128), jnp.float32)
    pairs(1, 2, whole=False)
    pairs(2, 3)
    pl.semaphore_wait(barrier, 16)
    start(comb_copies(0))
    pairs(3, (NB + 1) // 2)
    arrived(comb_copies(0))
    start(comb_copies(1))
    w_tail().wait()
    w[COLS:, :] = jnp.zeros((PADDED - COLS, D), jnp.bfloat16)
    running(NB - 2)
    running(NB - 1)
    logits[:, MAIN:] = lax.dot_general(h[...].reshape(TOK, D), w[MAIN:, :], NT, preferred_element_type=jnp.float32)
    running(NB, last=True)

    def original_rows(col, i):
        return jnp.concatenate([col[pl.ds(slot_of(8 * i + j) * OWN, OWN), :] for j in range(8)], axis=0)

    def lse_rows(i):
        peaks, sums = jnp.transpose(original_rows(top, i)), jnp.transpose(original_rows(total, i))
        peak = jnp.max(peaks, axis=0, keepdims=True)
        return peak + jnp.log(jnp.sum(sums * jnp.exp(peaks - peak), axis=0, keepdims=True))

    stat_core[0, core] = jnp.concatenate([lse_rows(i) for i in range(4)], axis=0)
    start(stat_copies(0, 0))

    arrived(comb_copies(1))
    pl.loop(0, 16, unroll=8)(target_rows)
    arrived(stat_copies(0, 0))
    stat_chip[0, z * 4 + y] = log_add(stat_core[0])
    start(stat_copies(0, 1))
    pl.loop(16, TOK // 8, unroll=8)(target_rows)
    arrived(stat_copies(0, 1))
    log_total = log_add(stat_chip[0])
    for i in range(4):
        col = jnp.transpose(jnp.broadcast_to(log_total[i:i + 1, :], (128, 128)))
        for j in range(8):
            ltcol[pl.ds(slot_of(8 * i + j) * OWN, OWN), :] = col[j * OWN:(j + 1) * OWN, :]

    @pl.loop(0, TOK // 16, unroll=2)
    def _(i):
        rows = pl.ds(pl.multiple_of(i * 16, 16), 16)
        lt = ltcol[rows, :]
        terms = jnp.zeros((16, 128), jnp.float32)
        for t in range(TILES):
            at = slice(t * 128, (t + 1) * 128)
            logit, want = logits[rows, at], target[rows, at]
            terms = terms + want * logit
            value = jnp.exp(logit - lt) - want
            if t == TILES - 1:
                value = jnp.where(lane < TAIL, value, jnp.float32(0.0))
            gm[rows, at] = value.astype(jnp.bfloat16)
        cross[rows, :] = terms

    own_rows = pl.ds(pl.multiple_of(my_slot * OWN, OWN), OWN)
    cross[own_rows, :] = cross[own_rows, :] - jnp.where(lane == 0, negent, jnp.float32(0.0))

    def multiply(unit):
        c = max(k for k in range(NC) if sum(CHUNKS[:k]) <= unit)
        at = (unit - sum(CHUNKS[:c])) * UNIT
        part = jnp.dot(gm[...], w[:, unit * UNIT:(unit + 1) * UNIT], preferred_element_type=jnp.float32)
        g[c][:, :, :, :, at:at + UNIT] = part.reshape(2, 4, 4, OWN, UNIT)

    def step_core(c):
        return [remote(g[c].at[1 - core], cr[c], g_send.at[c, 0], g_recv.at[c, 0], mate)]

    def step_far(c):
        far = (a + 2) % 4
        return [
            remote(g[c].at[core, far, 0:2], r11[c].at[0], g_send.at[c, 1], g_recv.at[c, 1], device(a_right, b)),
            remote(g[c].at[core, far, 2:4], r11[c].at[1], g_send.at[c, 2], g_recv.at[c, 2], device(a_left, b)),
        ]

    def step_near(c):
        return [
            remote(g[c].at[core, a_right], r12[c].at[0], g_send.at[c, 3], g_recv.at[c, 3], device(a_right, b)),
            remote(g[c].at[core, a_left], r12[c].at[1], g_send.at[c, 4], g_recv.at[c, 4], device(a_left, b)),
        ]

    def step_far2(c):
        if c in STRAIGHT:
            return [
                remote(g[c].at[core, a, (b + d) % 4], r2[c].at[d - 1], g_send.at[c, 4 + d], g_recv.at[c, 4 + d], device(a, (b + d) % 4))
                for d in (1, 2, 3)
            ]
        far = (b + 2) % 4
        return [
            remote(g[c].at[core, a, far, 0:8], r2[c].at[2, 0:8], g_send.at[c, 5], g_recv.at[c, 5], device(a, b_right)),
            remote(g[c].at[core, a, far, 8:16], r2[c].at[2, 8:16], g_send.at[c, 6], g_recv.at[c, 6], device(a, b_left)),
        ]

    def step_near2(c):
        return [
            remote(g[c].at[core, a, b_right], r2[c].at[0], g_send.at[c, 7], g_recv.at[c, 7], device(a, b_right)),
            remote(g[c].at[core, a, b_left], r2[c].at[1], g_send.at[c, 8], g_recv.at[c, 8], device(a, b_left)),
        ]

    unit = 0
    for event in ORDER:
        if event == "m":
            multiply(unit)
            unit += 1
            continue
        kind, c = event[0], int(event[1])
        if kind == "C":
            start(step_core(c))
        elif kind == "X":
            arrived(step_core(c))
            for k in range(4):
                g[c][core, k] = g[c][core, k] + cr[c][k]
            start(step_far(c))
        elif kind == "Y":
            arrived(step_far(c))
            g[c][core, a_right, 0:2] = g[c][core, a_right, 0:2] + r11[c][0]
            g[c][core, a_left, 2:4] = g[c][core, a_left, 2:4] + r11[c][1]
            start(step_near(c))
        elif kind == "Z":
            arrived(step_near(c))
            g[c][core, a] = g[c][core, a] + (r12[c][0] + r12[c][1])
            start(step_far2(c))
        elif kind == "W":
            arrived(step_far2(c))
            g[c][core, a, b_right, 0:8] = g[c][core, a, b_right, 0:8] + r2[c][2, 0:8]
            g[c][core, a, b_left, 8:16] = g[c][core, a, b_left, 8:16] + r2[c][2, 8:16]
            start(step_near2(c))
        elif kind == "F":
            arrived(step_far2(c) if c in STRAIGHT else step_near2(c))
            at = sum(CHUNKS[:c]) * UNIT
            value = g[c][core, a, b] + (r2[c][0] + r2[c][1])
            if c in STRAIGHT:
                value = value + r2[c][2]
            grad_out[:, at:at + CHUNKS[c] * UNIT] = value
        elif c == 1:
            rows = [jnp.sum(jnp.transpose(original_rows(cross, i)), axis=0, keepdims=True) for i in range(4)]
            stat_core[1, core] = jnp.concatenate(rows, axis=0)
            start(stat_copies(1, 0))
        elif c == 2:
            arrived(stat_copies(1, 0))
            stat_chip[1, z * 4 + y] = jnp.sum(stat_core[1], axis=0)
            start(stat_copies(1, 1))
        else:
            arrived(stat_copies(1, 1))
            loss_out[...] = log_total - jnp.sum(stat_chip[1], axis=0)

    for k in range(2):
        left(comb_copies(k) + stat_copies(0, k) + stat_copies(1, k))
    for c in range(NC):
        left(step_core(c) + step_far(c) + step_near(c) + step_far2(c) + ([] if c in STRAIGHT else step_near2(c)))


def finish(grad_ref, loss_ref, grad_out, loss_out):
    grad_out[...] = grad_ref[...]
    loss_out[...] = loss_ref[...]


def local(hidden, head_weight, teacher_ids, teacher_logits):
    any_space = pl.BlockSpec(memory_space=pl.ANY)
    vmem = pl.BlockSpec(memory_space=pltpu.VMEM)
    f32, bf16 = jnp.float32, jnp.bfloat16
    dma = pltpu.SemaphoreType.DMA
    widths = [k * UNIT for k in CHUNKS]
    grad, loss = pl.pallas_call(
        kernel,
        out_shape=(jax.ShapeDtypeStruct((OWN, D), f32), jax.ShapeDtypeStruct((4, 128), f32)),
        in_specs=[any_space] * 4,
        out_specs=(vmem, vmem),
        scratch_shapes=[
            pltpu.VMEM((PADDED, D), bf16),
            pltpu.VMEM((2, 4, 4, OWN, D), bf16),
            pltpu.VMEM((TOK, PADDED), f32),
            pltpu.VMEM((TOK, PADDED), f32),
            pltpu.VMEM((TOK, PADDED), bf16),
            [pltpu.VMEM((2, 4, 4, OWN, k), f32) for k in widths],
            [pltpu.VMEM((4, 4, OWN, k), f32) for k in widths],
            [pltpu.VMEM((2, 2, OWN, k), f32) for k in widths],
            [pltpu.VMEM((2, 4, OWN, k), f32) for k in widths],
            [pltpu.VMEM((3, OWN, k), f32) for k in widths],
            pltpu.VMEM((2, 4, 4, 4, 8 * K), f32),
            pltpu.VMEM((2, 2, 4, 128), f32),
            pltpu.VMEM((2, 16, 4, 128), f32),
            pltpu.VMEM((TOK, 128), f32),
            pltpu.VMEM((TOK, 128), f32),
            pltpu.VMEM((TOK, 128), f32),
            pltpu.VMEM((TOK, 128), f32),
            pltpu.VMEM((OWN, K), jnp.int32),
            pltpu.VMEM((OWN, K), f32),
            dma((2,)), dma, dma((NB + 1,)), dma((16,)), dma((16,)), dma((2, 16)), dma((2, 16)), dma((NC, 9)), dma((NC, 9)),
        ],
        compiler_params=pltpu.CompilerParams(
            collective_id=0, has_side_effects=True, vmem_limit_bytes=60 * 1024 * 1024),
    )(hidden.reshape(4, 4, 2, OWN, D), head_weight.T, teacher_ids, teacher_logits)
    grad, loss = pl.pallas_call(
        finish,
        out_shape=(jax.ShapeDtypeStruct((OWN, D), f32), jax.ShapeDtypeStruct((4, 128), f32)),
        in_specs=[vmem, vmem],
        out_specs=(vmem, vmem),
    )(grad, loss)
    return loss.reshape(TOK), grad


def solution(mesh):
    placed = (P("dp", None), P(None, "vocab"), P(("dp", "vocab"), None), P(("dp", "vocab"), None))
    return jax.shard_map(
        local,
        mesh=mesh,
        in_specs=placed,
        out_specs=(P("dp"), P(("dp", "vocab"), None)),
        check_vma=False,
    )
```

```python
import functools

import jax
import jax.numpy as jnp
from jax import lax
from jax.experimental import pallas as pl
from jax.experimental.pallas import tpu as pltpu
from jax.sharding import PartitionSpec as P

MESH = pl.DeviceIdType.MESH
NV = 32
TOK = 512
OWN = 16
D = 3584
COLS = 2376
MAIN = 2304
TAIL = COLS - MAIN
PADDED = MAIN + 128
TILES = PADDED // 128
NB = MAIN // 256
UNIT = 256
CHUNKS = (3, 4, 4, 3)
NC = len(CHUNKS)
STRAIGHT = (2, 3)
K = 64
ORDER = (
    "m", "m", "m", "C0", "m", "m", "X0", "m", "m", "C1", "m", "m", "X1", "Y0", "m", "m", "C2", "m", "m", "X2", "Y1", "m", "C3", "X3", "Y2", "K1", "Z0", "Y3", "Z1", "Z2", "W0", "K2", "Z3", "W1", "F0", "F1", "K3", "F2", "F3",
)
NT = (((1,), (1,)), ((), ()))


def slot_of(index):
    core, y, z = index % 2, (index // 2) % 4, index // 8
    return core * 16 + (y * 4 + z) * (1 - core) + (z * 4 + y) * core


def kernel(
    hidden, weight, ids_hbm, tlog_hbm,
    grad_out, loss_out,
    w, h, logits, target, gm, g, cr, r11, r12, r2,
    comb, stat_core, stat_chip, ltcol, top, total, cross,
    ids_ref, tlog_ref, t_sem, h_sem, w_sem, comb_send, comb_recv, st_send, st_recv, g_send, g_recv,
):
    me = lax.axis_index("vocab")
    core = me % 2
    y = (me // 2) % 4
    z = me // 8
    a = y * (1 - core) + z * core
    b = z * (1 - core) + y * core
    stride_a = 1 + 3 * core
    stride_b = 4 - 3 * core

    def device(a_pos, b_pos):
        return {"vocab": (a_pos * stride_a + b_pos * stride_b) * 2 + core}

    def chip(dy, dz):
        return {"vocab": (((z + dz) % 4) * 4 + (y + dy) % 4) * 2 + core}

    others = [(dy, dz) for dz in range(4) for dy in range(4) if dy or dz]

    def remote(src, dst, send, recv, where):
        return pltpu.make_async_remote_copy(src, dst, send, recv, device_id=where, device_id_type=MESH)

    mate = {"vocab": me + 1 - 2 * core}
    a_right, a_left = (a + 1) % 4, (a + 3) % 4
    b_right, b_left = (b + 1) % 4, (b + 3) % 4
    my_slot = core * 16 + a * 4 + b

    def start(copies):
        for copy in copies:
            copy.start()

    def arrived(copies):
        for copy in copies:
            copy.wait_recv()

    def left(copies):
        for copy in copies:
            copy.wait_send()

    def w_copy(n):
        rows = pl.ds(n * 256, 256)
        return pltpu.make_async_copy(weight.at[rows], w.at[rows], w_sem.at[n])

    def w_tail():
        rows = pl.ds(MAIN, TAIL)
        return pltpu.make_async_copy(weight.at[rows], w.at[rows], w_sem.at[NB])

    teacher = [
        pltpu.make_async_copy(ids_hbm, ids_ref, t_sem.at[0]),
        pltpu.make_async_copy(tlog_hbm, tlog_ref, t_sem.at[1]),
    ]
    start(teacher)
    w_copy(0).start()
    for k in range(4):
        pltpu.make_async_copy(hidden.at[:, k, 0], h.at[0, k], h_sem).start()
        pltpu.make_async_copy(hidden.at[k, :, 1], h.at[1, k], h_sem).start()
    for n in range(1, NB):
        w_copy(n).start()
    w_tail().start()

    barrier = pltpu.get_barrier_semaphore()
    for where in [mate] + [chip(dy, dz) for dy, dz in others]:
        pl.semaphore_signal(barrier, inc=1, device_id=where, device_id_type=MESH)
    for copy in teacher:
        copy.wait()
    tl = tlog_ref[...]
    shifted = tl - jnp.max(tl, axis=1, keepdims=True)
    log_probs = shifted - jnp.log(jnp.sum(jnp.exp(shifted), axis=1, keepdims=True))
    probs = jnp.exp(log_probs)
    negent = jnp.sum(probs * log_probs, axis=1, keepdims=True)
    ids = ids_ref[...].astype(jnp.float32)
    for i in range(2):
        for t in range(8):
            token = slice(i * 8 + t, i * 8 + t + 1)
            comb[core, z, y, i:i + 1, t * K:(t + 1) * K] = ids[token]
            comb[core, z, y, 2 + i:3 + i, t * K:(t + 1) * K] = probs[token]

    def comb_copies(k):
        if k == 1:
            return [remote(comb.at[core], comb.at[core], comb_send.at[15], comb_recv.at[15], mate)]
        block = comb.at[core, z, y]
        return [
            remote(block, block, comb_send.at[i], comb_recv.at[i], chip(dy, dz)) for i, (dy, dz) in enumerate(others)
        ]

    def stat_copies(which, k):
        if k == 0:
            block = stat_core.at[which, core]
            return [remote(block, block, st_send.at[which, 15], st_recv.at[which, 15], mate)]
        block = stat_chip.at[which, z * 4 + y]
        return [
            remote(block, block, st_send.at[which, i], st_recv.at[which, i], chip(dy, dz))
            for i, (dy, dz) in enumerate(others)
        ]

    def log_add(stats):
        peak = jnp.max(stats, axis=0)
        return peak + jnp.log(jnp.sum(jnp.exp(stats - peak[None]), axis=0))

    first = (me * COLS).astype(jnp.float32)
    bf16 = jnp.bfloat16
    row16 = lax.broadcasted_iota(jnp.int32, (16, 256), 0)
    lane256 = lax.broadcasted_iota(jnp.int32, (16, 256), 1)
    same_token = (row16 % 4) == (lane256 // K)
    tile_of_row = [
        (row16 // 4).astype(jnp.float32).astype(bf16),
        ((row16 // 4) ^ 1).astype(jnp.float32).astype(bf16),
    ]
    column_of_row = row16.astype(jnp.float32).astype(bf16)
    zero, one = jnp.zeros((16, 256), bf16), jnp.ones((16, 256), bf16)
    first_four = lax.broadcasted_iota(jnp.int32, (8, 128), 0) < 4

    def wide(row):
        return jnp.broadcast_to(row, (16, 256))

    def target_rows(i):
        rows = pl.ds(pl.multiple_of(i * 8, 8), 8)
        half, slot = i % 2, i // 2
        slot_core, outer, inner = slot // 16, (slot // 4) % 4, slot % 4
        slot_y = outer * (1 - slot_core) + inner * slot_core
        slot_z = inner * (1 - slot_core) + outer * slot_core
        offset = comb[slot_core, slot_z, slot_y, pl.ds(half, 1), :] - first
        inside = (offset >= 0) & (offset < COLS)
        tile = jnp.floor(offset * jnp.float32(1 / 128))
        column = offset - tile * 128
        tile = jnp.where(inside, tile, jnp.float32(-8))
        rest = comb[slot_core, slot_z, slot_y, pl.ds(2 + half, 1), :]
        parts = []
        for _ in range(3):
            parts.append(rest.astype(bf16).astype(jnp.float32))
            rest = rest - parts[-1]
        placed = []
        for k in range(2):
            at = slice(k * 256, (k + 1) * 256)
            tiles = jnp.where(same_token, wide(tile[:, at]), jnp.float32(-8)).astype(bf16) - tile_of_row[k]
            masks = [tiles == bf16(4 * j) for j in range(5)]
            left_side = [jnp.where(m, part, zero) for part in [wide(p[:, at]).astype(bf16) for p in parts] for m in masks]
            columns = wide(column[:, at]).astype(bf16) - column_of_row
            right_side = [jnp.where(columns == bf16(16 * j), one, zero) for j in range(8)]
            out = lax.dot_general(
                jnp.concatenate(left_side, axis=0), jnp.concatenate(right_side, axis=0), NT, preferred_element_type=jnp.float32)
            placed.append(out[0:80] + out[80:160] + out[160:240])
        for t in range(TILES):
            at, pair = slice(t * 128, (t + 1) * 128), slice(t // 2 * 8, t // 2 * 8 + 8)
            if t % 2 == 0:
                value = jnp.where(first_four, placed[0][pair], placed[1][pair])
            else:
                value = pltpu.roll(jnp.where(first_four, placed[1][pair], placed[0][pair]), 4, 0)
            target[rows, at] = value

    lane = lax.broadcasted_iota(jnp.int32, (16, 128), 1)

    def running(n, last=False):
        for r in range(0, TOK, 16):
            rows = slice(r, r + 16)
            values = [logits[rows, pl.ds(n * 256 if isinstance(n, int) else pl.multiple_of(n * 256, 256), 128)]]
            if last:
                values = [jnp.where(lane < TAIL, values[0], jnp.float32(-1e30))]
            else:
                at = n * 256 + 128
                values.append(logits[rows, pl.ds(at if isinstance(n, int) else pl.multiple_of(at, 128), 128)])
            peak = functools.reduce(jnp.maximum, values)
            old = top[rows, :]
            peak = jnp.maximum(old, peak)
            sums = functools.reduce(jnp.add, [jnp.exp(v - peak) for v in values])
            sums = sums + total[rows, :] * jnp.exp(old - peak)
            top[rows, :] = peak
            total[rows, :] = sums

    def logits_block(n, size):
        block = pl.ds(n * 256 if isinstance(n, int) else pl.multiple_of(n * 256, 256), size)
        logits[:, block] = lax.dot_general(h[...].reshape(TOK, D), w[block, :], NT, preferred_element_type=jnp.float32)

    def pairs(low, high, whole=True):
        @pl.loop(low, high)
        def _(k):
            w_copy(2 * k - 1).wait()
            w_copy(2 * k).wait()
            if whole:
                running(2 * k - 3)
            running(2 * k - 2)
            logits_block(2 * k - 1, 512)

    pltpu.make_async_copy(h, h, h_sem).wait()
    w_copy(0).wait()
    logits_block(0, 256)
    top[...] = jnp.full((TOK, 128), -1e30, jnp.float32)
    total[...] = jnp.zeros((TOK, 128), jnp.float32)
    pairs(1, 2, whole=False)
    pairs(2, 3)
    pl.semaphore_wait(barrier, 16)
    start(comb_copies(0))
    pairs(3, (NB + 1) // 2)
    arrived(comb_copies(0))
    start(comb_copies(1))
    w_tail().wait()
    w[COLS:, :] = jnp.zeros((PADDED - COLS, D), jnp.bfloat16)
    running(NB - 2)
    running(NB - 1)
    logits[:, MAIN:] = lax.dot_general(h[...].reshape(TOK, D), w[MAIN:, :], NT, preferred_element_type=jnp.float32)
    running(NB, last=True)

    def original_rows(col, i):
        return jnp.concatenate([col[pl.ds(slot_of(8 * i + j) * OWN, OWN), :] for j in range(8)], axis=0)

    def lse_rows(i):
        peaks, sums = jnp.transpose(original_rows(top, i)), jnp.transpose(original_rows(total, i))
        peak = jnp.max(peaks, axis=0, keepdims=True)
        return peak + jnp.log(jnp.sum(sums * jnp.exp(peaks - peak), axis=0, keepdims=True))

    stat_core[0, core] = jnp.concatenate([lse_rows(i) for i in range(4)], axis=0)
    start(stat_copies(0, 0))

    arrived(comb_copies(1))
    pl.loop(0, 8, unroll=8)(target_rows)
    arrived(stat_copies(0, 0))
    stat_chip[0, z * 4 + y] = log_add(stat_core[0])
    start(stat_copies(0, 1))
    pl.loop(8, TOK // 8, unroll=8)(target_rows)
    arrived(stat_copies(0, 1))
    log_total = log_add(stat_chip[0])
    for i in range(4):
        col = jnp.transpose(jnp.broadcast_to(log_total[i:i + 1, :], (128, 128)))
        for j in range(8):
            ltcol[pl.ds(slot_of(8 * i + j) * OWN, OWN), :] = col[j * OWN:(j + 1) * OWN, :]

    @pl.loop(0, TOK // 16, unroll=2)
    def _(i):
        rows = pl.ds(pl.multiple_of(i * 16, 16), 16)
        lt = ltcol[rows, :]
        terms = jnp.zeros((16, 128), jnp.float32)
        for t in range(TILES):
            at = slice(t * 128, (t + 1) * 128)
            logit, want = logits[rows, at], target[rows, at]
            terms = terms + want * logit
            value = jnp.exp(logit - lt) - want
            if t == TILES - 1:
                value = jnp.where(lane < TAIL, value, jnp.float32(0.0))
            gm[rows, at] = value.astype(jnp.bfloat16)
        cross[rows, :] = terms

    own_rows = pl.ds(pl.multiple_of(my_slot * OWN, OWN), OWN)
    cross[own_rows, :] = cross[own_rows, :] - jnp.where(lane == 0, negent, jnp.float32(0.0))

    def multiply(unit):
        c = max(k for k in range(NC) if sum(CHUNKS[:k]) <= unit)
        at = (unit - sum(CHUNKS[:c])) * UNIT
        part = jnp.dot(gm[...], w[:, unit * UNIT:(unit + 1) * UNIT], preferred_element_type=jnp.float32)
        g[c][:, :, :, :, at:at + UNIT] = part.reshape(2, 4, 4, OWN, UNIT)

    def step_core(c):
        return [remote(g[c].at[1 - core], cr[c], g_send.at[c, 0], g_recv.at[c, 0], mate)]

    def step_far(c):
        far = (a + 2) % 4
        return [
            remote(g[c].at[core, far, 0:2], r11[c].at[0], g_send.at[c, 1], g_recv.at[c, 1], device(a_right, b)),
            remote(g[c].at[core, far, 2:4], r11[c].at[1], g_send.at[c, 2], g_recv.at[c, 2], device(a_left, b)),
        ]

    def step_near(c):
        return [
            remote(g[c].at[core, a_right], r12[c].at[0], g_send.at[c, 3], g_recv.at[c, 3], device(a_right, b)),
            remote(g[c].at[core, a_left], r12[c].at[1], g_send.at[c, 4], g_recv.at[c, 4], device(a_left, b)),
        ]

    def step_far2(c):
        if c in STRAIGHT:
            return [
                remote(g[c].at[core, a, (b + d) % 4], r2[c].at[d - 1], g_send.at[c, 4 + d], g_recv.at[c, 4 + d], device(a, (b + d) % 4))
                for d in (1, 2, 3)
            ]
        far = (b + 2) % 4
        return [
            remote(g[c].at[core, a, far, 0:8], r2[c].at[2, 0:8], g_send.at[c, 5], g_recv.at[c, 5], device(a, b_right)),
            remote(g[c].at[core, a, far, 8:16], r2[c].at[2, 8:16], g_send.at[c, 6], g_recv.at[c, 6], device(a, b_left)),
        ]

    def step_near2(c):
        return [
            remote(g[c].at[core, a, b_right], r2[c].at[0], g_send.at[c, 7], g_recv.at[c, 7], device(a, b_right)),
            remote(g[c].at[core, a, b_left], r2[c].at[1], g_send.at[c, 8], g_recv.at[c, 8], device(a, b_left)),
        ]

    unit = 0
    for event in ORDER:
        if event == "m":
            multiply(unit)
            unit += 1
            continue
        kind, c = event[0], int(event[1])
        if kind == "C":
            start(step_core(c))
        elif kind == "X":
            arrived(step_core(c))
            for k in range(4):
                g[c][core, k] = g[c][core, k] + cr[c][k]
            start(step_far(c))
        elif kind == "Y":
            arrived(step_far(c))
            g[c][core, a_right, 0:2] = g[c][core, a_right, 0:2] + r11[c][0]
            g[c][core, a_left, 2:4] = g[c][core, a_left, 2:4] + r11[c][1]
            start(step_near(c))
        elif kind == "Z":
            arrived(step_near(c))
            g[c][core, a] = g[c][core, a] + (r12[c][0] + r12[c][1])
            start(step_far2(c))
        elif kind == "W":
            arrived(step_far2(c))
            g[c][core, a, b_right, 0:8] = g[c][core, a, b_right, 0:8] + r2[c][2, 0:8]
            g[c][core, a, b_left, 8:16] = g[c][core, a, b_left, 8:16] + r2[c][2, 8:16]
            start(step_near2(c))
        elif kind == "F":
            arrived(step_far2(c) if c in STRAIGHT else step_near2(c))
            at = sum(CHUNKS[:c]) * UNIT
            value = g[c][core, a, b] + (r2[c][0] + r2[c][1])
            if c in STRAIGHT:
                value = value + r2[c][2]
            grad_out[:, at:at + CHUNKS[c] * UNIT] = value
        elif c == 1:
            rows = [jnp.sum(jnp.transpose(original_rows(cross, i)), axis=0, keepdims=True) for i in range(4)]
            stat_core[1, core] = jnp.concatenate(rows, axis=0)
            start(stat_copies(1, 0))
        elif c == 2:
            arrived(stat_copies(1, 0))
            stat_chip[1, z * 4 + y] = jnp.sum(stat_core[1], axis=0)
            start(stat_copies(1, 1))
        else:
            arrived(stat_copies(1, 1))
            loss_out[...] = log_total - jnp.sum(stat_chip[1], axis=0)

    for k in range(2):
        left(comb_copies(k) + stat_copies(0, k) + stat_copies(1, k))
    for c in range(NC):
        left(step_core(c) + step_far(c) + step_near(c) + step_far2(c) + ([] if c in STRAIGHT else step_near2(c)))


def finish(grad_ref, loss_ref, grad_out, loss_out):
    grad_out[...] = grad_ref[...]
    loss_out[...] = loss_ref[...]


def local(hidden, head_weight, teacher_ids, teacher_logits):
    any_space = pl.BlockSpec(memory_space=pl.ANY)
    vmem = pl.BlockSpec(memory_space=pltpu.VMEM)
    f32, bf16 = jnp.float32, jnp.bfloat16
    dma = pltpu.SemaphoreType.DMA
    widths = [k * UNIT for k in CHUNKS]
    grad, loss = pl.pallas_call(
        kernel,
        out_shape=(jax.ShapeDtypeStruct((OWN, D), f32), jax.ShapeDtypeStruct((4, 128), f32)),
        in_specs=[any_space] * 4,
        out_specs=(vmem, vmem),
        scratch_shapes=[
            pltpu.VMEM((PADDED, D), bf16),
            pltpu.VMEM((2, 4, 4, OWN, D), bf16),
            pltpu.VMEM((TOK, PADDED), f32),
            pltpu.VMEM((TOK, PADDED), f32),
            pltpu.VMEM((TOK, PADDED), bf16),
            [pltpu.VMEM((2, 4, 4, OWN, k), f32) for k in widths],
            [pltpu.VMEM((4, 4, OWN, k), f32) for k in widths],
            [pltpu.VMEM((2, 2, OWN, k), f32) for k in widths],
            [pltpu.VMEM((2, 4, OWN, k), f32) for k in widths],
            [pltpu.VMEM((3, OWN, k), f32) for k in widths],
            pltpu.VMEM((2, 4, 4, 4, 8 * K), f32),
            pltpu.VMEM((2, 2, 4, 128), f32),
            pltpu.VMEM((2, 16, 4, 128), f32),
            pltpu.VMEM((TOK, 128), f32),
            pltpu.VMEM((TOK, 128), f32),
            pltpu.VMEM((TOK, 128), f32),
            pltpu.VMEM((TOK, 128), f32),
            pltpu.VMEM((OWN, K), jnp.int32),
            pltpu.VMEM((OWN, K), f32),
            dma((2,)), dma, dma((NB + 1,)), dma((16,)), dma((16,)), dma((2, 16)), dma((2, 16)), dma((NC, 9)), dma((NC, 9)),
        ],
        compiler_params=pltpu.CompilerParams(
            collective_id=0, has_side_effects=True, vmem_limit_bytes=60 * 1024 * 1024),
    )(hidden.reshape(4, 4, 2, OWN, D), head_weight.T, teacher_ids, teacher_logits)
    grad, loss = pl.pallas_call(
        finish,
        out_shape=(jax.ShapeDtypeStruct((OWN, D), f32), jax.ShapeDtypeStruct((4, 128), f32)),
        in_specs=[vmem, vmem],
        out_specs=(vmem, vmem),
    )(grad, loss)
    return loss.reshape(TOK), grad


def solution(mesh):
    placed = (P("dp", None), P(None, "vocab"), P(("dp", "vocab"), None), P(("dp", "vocab"), None))
    return jax.shard_map(
        local,
        mesh=mesh,
        in_specs=placed,
        out_specs=(P("dp"), P(("dp", "vocab"), None)),
        check_vma=False,
    )
```
